32 devices in a mesh: pool: 2 (over y), dp: 8 (over z, x), tensor: 2 (over core).
Axes of the slice: x: 2, y: 2, z: 4, core: 2. Of those that a mesh axis runs over, the one named last changes fastest.
Arguments:
- train_out: bfloat16 [2048, 4096], P(('pool', 'dp'), 'tensor'), parts along dimension 0, may hold values from -3 to 3
- train_in: bfloat16 [2048, 14336], P(('pool', 'dp'), 'tensor'), parts along dimension 0, may hold values from -6 to 6
- query_out: bfloat16 [128, 4096], P(None, 'dp'), may hold values from -0.08984375 to 0.08984375
- query_in: bfloat16 [128, 14336], P('dp', 'tensor'), may hold values from -0.044921875 to 0.044921875
- basis_out: bfloat16 [4096, 4096], P('dp', 'tensor'), may hold values from -0.09375 to 0.09375
- basis_in: bfloat16 [14336, 14336], P('tensor', 'dp'), may hold values from -0.046875 to 0.046875
- eigval: bfloat16 [4096, 14336], P('tensor', 'dp'), may hold values from 0.049804688 to 5
- sketch_bucket: int32 [14336], P('dp'), may hold values from 0 to 7
- sketch_sign: int32 [14336], P('dp'), may hold values from 0 to 1
- lengths: int32 [16, 4], P(('pool', 'dp')), parts along dimension 0, may hold values from 1 to 64, 128 in all within a row
- source_of_seq: int32 [64], P(('pool', 'dp')), parts along dimension 0, may hold values from 0 to 31
Outputs:
- scores: float32 [64, 8], P(('pool', 'dp')), parts along dimension 0
- source_totals: float32 [64, 8], P('pool'), parts along dimension 0
The draws below stay inside these ranges and needn't reach their ends.
There are 2 independent parts, one for each index of `pool`. The reference program is written for one: setup_inputs(seed, part) draws one part's arguments, and reference() takes and returns one part's arrays. A program takes and returns all parts, laid end to end along the dimension named above; an argument that names none is the same for every part. Nothing has to cross between parts.
Inputs may be any that keep to these rules, and one draw needn't show every extreme that they name: `lengths`: row j holds the token counts of the 4 sequences of dp index j in order; each row sums to 128 and its largest count is half of 128.
All inputs are finite; a program needn't handle non-finite values.
Results may differ from the reference program's by a relative error of at most 0.0003.
Values may be sent and summed in bfloat16 or wider, within the bound.
A program may use at most 320 MiB of HBM per device.

```python
import math
import jax
import jax.numpy as jnp
import numpy as np
from jax import lax

D = 4096
FF = 14336
TOK_DEV = 128
SEQ_DEV = 4
QUERIES = 8
QLEN = 16
RANK = 8
SOURCES = 32
TOKENS = 1024
SEQS = 32
QTOK = 128
N_DP = 8


def touch_ends(result, own_key, smallest, top_value):
    spot = [jax.random.randint(jax.random.fold_in(own_key, axis), (), 0, length) for axis, length in enumerate(result.shape)]
    main_axis = result.shape.index(max(result.shape))
    next_to = spot[:main_axis] + [(spot[main_axis] + 1) % result.shape[main_axis]] + spot[main_axis + 1:]
    return result.at[tuple(spot)].set(smallest).at[tuple(next_to)].set(top_value)


def shard_levels(stream_key, dims, shards, low, largest):
    loudness = 1.0
    for axis_at, blocks in shards:
        draws = jax.random.uniform(jax.random.fold_in(jax.random.fold_in(stream_key, 6), axis_at), (blocks,), jnp.float32, low / len(shards), largest / len(shards))
        loudness = loudness * jnp.repeat(jnp.exp(draws), dims[axis_at] // blocks).reshape((-1,) + (1,) * (len(dims) - 1 - axis_at))
    return loudness


def length_profile(count, total, reach, lean):
    portions = [(1 << 20) // math.isqrt(grade ** lean) + 1 for grade in range(2, count + 1)]
    rest, given = total - reach - (count - 1), [1] * (count - 1)
    while rest > 0:
        free = [i for i in range(count - 1) if given[i] < reach]
        pool, budget = sum([portions[i] for i in free]), rest
        for i in free:
            extra = min(reach - given[i], max(1, budget * portions[i] // pool), rest)
            given[i] = given[i] + extra
            rest = rest - extra
    return np.array([reach] + given)


def uneven_parts(key, amount, total, limit, slope):
    if amount == 2:
        one = jax.random.randint(key, (), max(1, total - limit), min(limit, total - 1) + 1)
        return jnp.stack([one, total - one])
    tallies = jnp.asarray(length_profile(amount, total, limit, slope), jnp.int32)
    couples = (amount - 1) // 2
    donor, sink = tallies[1:1 + 2 * couples:2], tallies[2:2 + 2 * couples:2]
    slack = jnp.minimum(donor - 1, limit - sink)
    passed = jax.random.randint(jax.random.fold_in(key, 1), (couples,), 0, 1 << 20) % (slack + 1)
    tallies = tallies.at[1:1 + 2 * couples:2].set(donor - passed).at[2:2 + 2 * couples:2].set(sink + passed)
    return tallies[jax.random.permutation(jax.random.fold_in(key, 2), amount)]


def normal_values(key, shape, spread, reach, pieces=(), kind=jnp.bfloat16):
    values = spread * jax.random.normal(key, shape, jnp.float32)
    if pieces:
        values = values * shard_levels(key, shape, pieces, -0.22, 0.18)
    return jnp.clip(values, -reach, reach).astype(kind)


def setup_inputs(seed: int = 0, part: int = 0) -> dict:
    key_list = jax.random.split(jax.random.key(seed), 12)
    part_keys = jax.random.split(jax.random.fold_in(key_list[11], part), 12)
    train_out = normal_values(part_keys[0], (TOKENS, D), 0.5, 3.0, ((0, 8), (1, 2)))
    train_in = normal_values(part_keys[1], (TOKENS, FF), 1.0, 6.0, ((0, 8), (1, 2)))
    query_out = normal_values(key_list[2], (QTOK, D), 0.015625, 0.08984375, ((1, 8),))
    query_in = normal_values(key_list[3], (QTOK, FF), 0.0078125, 0.044921875, ((0, 8), (1, 2)))
    basis_out = normal_values(key_list[4], (D, D), D ** -0.5, 0.09375, ((0, 8), (1, 2)))
    basis_in = normal_values(key_list[5], (FF, FF), FF ** -0.5, 0.046875, ((0, 2), (1, 8)))
    eigval = jnp.clip(jnp.exp(math.log(5.0) - 4.609084 * jax.random.uniform(key_list[6], (D, FF), jnp.float32) ** shard_levels(key_list[6], (D, FF), ((0, 2), (1, 8)), -0.2, 0.2)), 0.049804688, 5.0).astype(jnp.bfloat16)
    sketch_bucket = touch_ends(jax.random.randint(key_list[7], (FF,), 0, RANK), jax.random.fold_in(key_list[7], 1), 0, RANK - 1).astype(jnp.int32)
    sketch_sign = touch_ends(jax.random.randint(key_list[8], (FF,), 0, 2), jax.random.fold_in(key_list[8], 1), 0, 1).astype(jnp.int32)
    lengths = jax.vmap(lambda own: uneven_parts(own, SEQ_DEV, TOK_DEV, TOK_DEV // 2, 0))(jax.random.split(part_keys[9], N_DP)).reshape((N_DP, SEQ_DEV)).astype(jnp.int32)
    source_of_seq = touch_ends(jax.random.randint(part_keys[10], (SEQS,), 0, SOURCES), jax.random.fold_in(part_keys[10], 1), 0, SOURCES - 1).astype(jnp.int32)
    return {"train_out": train_out, "train_in": train_in, "query_out": query_out, "query_in": query_in, "basis_out": basis_out, "basis_in": basis_in, "eigval": eigval, "sketch_bucket": sketch_bucket, "sketch_sign": sketch_sign, "lengths": lengths, "source_of_seq": source_of_seq}


DAMP = 0.1

def sketch_table(bucket_ids, sign_bits):
    column_ids = jnp.arange(RANK, dtype=jnp.int32)
    signs = (2 * sign_bits - 1).astype(jnp.float32)
    return jnp.where(bucket_ids[:, None] == column_ids[None, :], signs[:, None], jnp.float32(0.0))

def query_factors(out_block, in_block, eig_plus, sketch):
    precond = jnp.dot(out_block, in_block, precision=lax.Precision.HIGHEST) / eig_plus
    sketched = jnp.dot(precond, sketch, precision=lax.Precision.HIGHEST)
    gram_matrix = jnp.dot(sketched.T, sketched, precision=lax.Precision.HIGHEST)
    chol_factor = jnp.linalg.cholesky(gram_matrix)
    left_trans = jax.scipy.linalg.solve_triangular(chol_factor, sketched.T, lower=True)
    right_trans = jnp.dot(left_trans, precond, precision=lax.Precision.HIGHEST)
    return (left_trans, right_trans)

def reference(train_out, train_in, query_out, query_in, basis_out, basis_in, eigval, sketch_bucket, sketch_sign, lengths, source_of_seq):
    rotated_out = lax.dot_general(basis_out.astype(jnp.float32), query_out.astype(jnp.float32), (((0,), (1,)), ((), ())), preferred_element_type=jnp.float32)
    rotated_in = jnp.dot(query_in.astype(jnp.float32), basis_in.astype(jnp.float32), preferred_element_type=jnp.float32)
    eig_plus = eigval.astype(jnp.float32) + DAMP
    sketch = sketch_table(sketch_bucket, sketch_sign)
    out_blocks = jnp.transpose(rotated_out.reshape(D, QUERIES, QLEN), (1, 0, 2))
    in_blocks = rotated_in.reshape(QUERIES, QLEN, FF)

    def one_query(pair):
        return query_factors(pair[0], pair[1], eig_plus, sketch)
    left_trans, right_trans = lax.map(one_query, (out_blocks, in_blocks))
    left_eig = jnp.transpose(left_trans, (2, 0, 1)).reshape(D, QUERIES * RANK)
    right_eig = jnp.transpose(right_trans, (2, 0, 1)).reshape(FF, QUERIES * RANK)
    left_factor = jnp.dot(basis_out.astype(jnp.float32), left_eig, precision=lax.Precision.HIGHEST)
    right_factor = jnp.dot(basis_in.astype(jnp.float32), right_eig, precision=lax.Precision.HIGHEST)
    proj_out = jnp.dot(train_out.astype(jnp.float32), left_factor, precision=lax.Precision.HIGHEST)
    proj_in = jnp.dot(train_in.astype(jnp.float32), right_factor, precision=lax.Precision.HIGHEST)
    token_score = (proj_out * proj_in).reshape(N_DP, TOK_DEV, QUERIES, RANK).sum(axis=3)
    seq_ends = jnp.cumsum(lengths, axis=1)
    seq_starts = seq_ends - lengths
    positions = jnp.arange(TOK_DEV, dtype=jnp.int32)
    member = ((positions[None, None, :] >= seq_starts[:, :, None]) & (positions[None, None, :] < seq_ends[:, :, None])).astype(jnp.float32)
    seq_sum = jnp.einsum('jst,jtq->jsq', member, token_score, precision=lax.Precision.HIGHEST)
    scores = (seq_sum / lengths.astype(jnp.float32)[:, :, None]).reshape(SEQS, QUERIES)
    owner_table = (source_of_seq[None, :] == jnp.arange(SOURCES, dtype=jnp.int32)[:, None]).astype(jnp.float32)
    source_totals = jnp.dot(owner_table, scores, precision=lax.Precision.HIGHEST)
    return (scores, source_totals)
```

```python
import functools

import jax
import jax.numpy as jnp
from jax import lax
from jax.experimental import pallas as pl
from jax.experimental.pallas import tpu as pltpu
from jax.sharding import PartitionSpec as P

QUERIES = 8
QLEN = 16
RANK = 8
SOURCES = 32


DAMP = 0.1

F32 = jnp.float32
BF16 = jnp.bfloat16
MESH = pl.DeviceIdType.MESH
NT = (((1,), (1,)), ((), ()))
NN = (((1,), (0,)), ((), ()))
HALF_Q = QUERIES // 2
HALF_TOK = HALF_Q * QLEN
HALF_COLS = HALF_Q * RANK
VMEM = pl.BlockSpec(memory_space=pltpu.VMEM)


def split(x):
    hi = x.astype(BF16)
    return hi, (x - hi.astype(F32)).astype(BF16)


def mm(a, b, dims):
    return lax.dot_general(a, b, dims, preferred_element_type=F32)


def greet(targets):
    barrier = pltpu.get_barrier_semaphore()
    for target in targets:
        pl.semaphore_signal(barrier, inc=1, device_id=target, device_id_type=MESH)
    pl.semaphore_wait(barrier, len(targets))


def remote(src, dst, send, recv, target):
    return pltpu.make_async_remote_copy(
        src_ref=src, dst_ref=dst, send_sem=send, recv_sem=recv,
        device_id=target, device_id_type=MESH,
    )


def params(collective_id):
    return pltpu.CompilerParams(
        collective_id=collective_id, has_side_effects=True, vmem_limit_bytes=56 << 20
    )


def gather_kernel(n, qin, part, q_all, a_out, recv, q_send, q_recv, rs_send, rs_recv, ag_send, ag_recv):
    d = lax.axis_index("dp")
    p = lax.axis_index("pool")
    rows = part.shape[0] // n
    peers = [lax.rem(d + k, n) for k in range(n)]
    greet([{"dp": peers[k]} for k in range(1, n)])

    def scatter(k):
        return remote(
            part.at[pl.ds(pl.multiple_of(peers[k] * rows, rows), rows)], recv.at[k],
            rs_send.at[k], rs_recv.at[k], {"dp": peers[k]},
        )

    for k in range(1, n):
        scatter(k).start()
    mine = d // 2
    is_sender = d == 2 * mine + lax.rem(mine + p, 2)

    def query_copy(j, k):
        return remote(
            qin, q_all.at[pl.ds(pl.multiple_of(j * QLEN, QLEN), QLEN)],
            q_send.at[k], q_recv.at[j], {"dp": peers[k]},
        )

    @pl.when(is_sender)
    def _():
        for k in range(1, n):
            query_copy(mine, k).start()
        q_all[pl.ds(pl.multiple_of(mine * QLEN, QLEN), QLEN), :] = qin[...]

    for k in range(1, n):
        scatter(k).wait_recv()
    own = pl.ds(pl.multiple_of(d * rows, rows), rows)
    total = part[own, :]
    for k in range(1, n):
        total = total + recv[k]
    a_out[own, :] = total

    def share(k):
        return remote(a_out.at[own], a_out.at[own], ag_send.at[k], ag_recv.at[k], {"dp": peers[k]})

    for k in range(1, n):
        share(k).start()
    for k in range(1, n):
        source = lax.rem(d + n - k, n)
        theirs = pl.ds(pl.multiple_of(source * rows, rows), rows)
        remote(a_out.at[own], a_out.at[theirs], ag_send.at[k], ag_recv.at[k], {"dp": peers[k]}).wait_recv()
        scatter(k).wait_send()
        share(k).wait_send()
    for j in range(HALF_Q):
        @pl.when(d != 2 * j + lax.rem(j + p, 2))
        def _():
            query_copy(j, 1).wait_recv()

    @pl.when(is_sender)
    def _():
        for k in range(1, n):
            query_copy(mine, k).wait_send()


def gather(n, query_in, out_part):
    dma = pltpu.SemaphoreType.DMA
    return pl.pallas_call(
        functools.partial(gather_kernel, n),
        out_shape=(
            jax.ShapeDtypeStruct((HALF_TOK, query_in.shape[1]), BF16),
            jax.ShapeDtypeStruct(out_part.shape, F32),
        ),
        in_specs=[VMEM] * 2,
        out_specs=(VMEM, VMEM),
        scratch_shapes=[
            pltpu.VMEM((n, out_part.shape[0] // n, out_part.shape[1]), F32),
            dma((n,)), dma((HALF_Q,)), dma((n,)), dma((n,)), dma((n,)), dma((n,)),
        ],
        compiler_params=params(0),
    )(query_in, out_part)


def rotate_kernel(tiles, q_all, basis, out, part, recv, send_sem, recv_sem):
    i = pl.program_id(0)
    partner = {"tensor": 1 - lax.axis_index("tensor")}

    @pl.when(i == 0)
    def _():
        greet([partner])

    part[i] = mm(q_all[...], basis[...], NN)
    remote(part.at[i], recv.at[i], send_sem.at[i], recv_sem.at[i], partner).start()

    @pl.when(i == tiles - 1)
    def _():
        width = part.shape[2]
        for j in range(tiles):
            remote(part.at[j], recv.at[j], send_sem.at[j], recv_sem.at[j], partner).wait()
            out[:, j * width:(j + 1) * width] = part[j] + recv[j]


def rotate(q_all, basis_in, width):
    depth, cols = basis_in.shape
    rows = q_all.shape[0]
    tiles = cols // width
    dma = pltpu.SemaphoreType.DMA
    return pl.pallas_call(
        functools.partial(rotate_kernel, tiles),
        grid=(tiles,),
        out_shape=jax.ShapeDtypeStruct((rows, cols), F32),
        in_specs=[
            pl.BlockSpec((rows, depth), lambda i: (0, 0)),
            pl.BlockSpec((depth, width), lambda i: (0, i)),
        ],
        out_specs=pl.BlockSpec((rows, cols), lambda i: (0, 0)),
        scratch_shapes=[
            pltpu.VMEM((tiles, rows, width), F32), pltpu.VMEM((tiles, rows, width), F32),
            dma((tiles,)), dma((tiles,)),
        ],
        compiler_params=params(1),
    )(q_all, basis_in)


def sketch_kernel(
    n, b_ref, bucket, sign, eig, a_ref, left, bs_hi, bs_lo, part, recv, whole, gram_mine, gram_theirs,
    rs_send, rs_recv, ag_send, ag_recv, g_sem,
):
    i = pl.program_id(0)
    d = lax.axis_index("dp")
    partner = {"tensor": 1 - lax.axis_index("tensor")}

    @pl.when(i == 0)
    def _():
        greet([{"dp": lax.rem(d + k, n)} for k in range(1, n)] + [partner])
        signs = (2 * sign[...] - 1).astype(F32)
        for k in range(RANK):
            table = jnp.where(bucket[...] == k, signs, 0.0)
            hi, lo = split(b_ref[...] * table)
            bs_hi[k * HALF_TOK:(k + 1) * HALF_TOK, :] = hi
            bs_lo[k * HALF_TOK:(k + 1) * HALF_TOK, :] = lo

    r_hi, r_lo = split(1.0 / (eig[...].astype(F32) + DAMP))
    prod = mm(bs_hi[...], r_hi, NT) + mm(bs_lo[...], r_hi, NT) + mm(bs_hi[...], r_lo, NT)
    width = eig.shape[0]
    for k in range(RANK):
        block = prod[k * HALF_TOK:(k + 1) * HALF_TOK] * a_ref[...]
        part[i, k * HALF_Q:(k + 1) * HALF_Q, :] = block.reshape(HALF_Q, QLEN, width).sum(axis=1)

    def scatter(k):
        to = lax.rem(d + k, n)
        return remote(part.at[to], recv.at[k], rs_send.at[k], rs_recv.at[k], {"dp": to})

    @pl.when(i != d)
    def _():
        k = lax.rem(i - d + n, n)
        remote(part.at[i], recv.at[k], rs_send.at[k], rs_recv.at[k], {"dp": i}).start()

    @pl.when(i == n - 1)
    def _():
        total = part[d]
        for k in range(1, n):
            scatter(k).wait_recv()
            total = total + recv[k]
        whole[d] = total
        for k in range(1, n):
            to = lax.rem(d + k, n)
            remote(whole.at[d], whole.at[d], ag_send.at[k], ag_recv.at[k], {"dp": to}).start()
        for k in range(1, n):
            to, source = lax.rem(d + k, n), lax.rem(d + n - k, n)
            remote(whole.at[d], whole.at[source], ag_send.at[k], ag_recv.at[k], {"dp": to}).wait()
            scatter(k).wait_send()
        rows = [
            jnp.concatenate([whole[c, k * HALF_Q:(k + 1) * HALF_Q, :] for c in range(n)], axis=1)
            for k in range(RANK)
        ]
        lane = lax.broadcasted_iota(jnp.int32, (HALF_Q, 128), 1)
        packed = jnp.zeros((HALF_Q, 128), F32)
        for r in range(RANK):
            for k in range(r + 1):
                dot = jnp.sum(rows[r] * rows[k], axis=1, keepdims=True)
                packed = jnp.where(lane == r * RANK + k, dot, packed)
        gram_mine[0:HALF_Q, :] = packed
        gram_mine[HALF_Q:2 * HALF_Q, :] = packed
        copy = remote(gram_mine, gram_theirs, g_sem.at[0], g_sem.at[1], partner)
        copy.start()
        copy.wait()
        gram = gram_mine[0:HALF_Q, :] + gram_theirs[0:HALF_Q, :]
        low = [[None] * RANK for _ in range(RANK)]
        done = []
        for r in range(RANK):
            for k in range(r + 1):
                value = gram[:, r * RANK + k:r * RANK + k + 1]
                for m in range(k):
                    value = value - low[r][m] * low[k][m]
                low[r][k] = jnp.sqrt(value) if k == r else value / low[k][k]
            row = rows[r]
            for k in range(r):
                row = row - low[r][k] * done[k]
            row = row / low[r][r]
            done.append(row)
            left[r * HALF_Q:(r + 1) * HALF_Q, :] = row


def sketch_left(n, b, bucket, sign, eigval, a):
    own_rows, cols = eigval.shape
    width = own_rows // n
    toks = b.shape[0]
    dma = pltpu.SemaphoreType.DMA
    fixed = lambda i: (0, 0)
    return pl.pallas_call(
        functools.partial(sketch_kernel, n),
        grid=(n,),
        out_shape=jax.ShapeDtypeStruct((HALF_COLS, own_rows), F32),
        in_specs=[
            pl.BlockSpec((toks, cols), fixed),
            pl.BlockSpec((1, cols), fixed),
            pl.BlockSpec((1, cols), fixed),
            pl.BlockSpec((width, cols), lambda i: (i, 0)),
            pl.BlockSpec((toks, width), lambda i: (0, i)),
        ],
        out_specs=pl.BlockSpec((HALF_COLS, own_rows), fixed),
        scratch_shapes=[
            pltpu.VMEM((RANK * toks, cols), BF16), pltpu.VMEM((RANK * toks, cols), BF16),
            pltpu.VMEM((n, HALF_COLS, width), F32), pltpu.VMEM((n, HALF_COLS, width), F32),
            pltpu.VMEM((n, HALF_COLS, width), F32),
            pltpu.VMEM((2 * HALF_Q, 128), F32), pltpu.VMEM((2 * HALF_Q, 128), F32),
            dma((n,)), dma((n,)), dma((n,)), dma((n,)), dma((2,)),
        ],
        compiler_params=params(2),
    )(b, bucket, sign, eigval, a)


def right_kernel(tiles, left, a_ref, eig, b_ref, out, al_hi, al_lo, part, recv, send_sem, recv_sem):
    i = pl.program_id(0)
    partner = {"tensor": 1 - lax.axis_index("tensor")}
    depth = left.shape[1]

    @pl.when(i == 0)
    def _():
        greet([partner])
        for r in range(RANK):
            for j in range(HALF_Q):
                at = r * HALF_Q + j
                hi, lo = split(left[at:at + 1, :] * a_ref[j * QLEN:(j + 1) * QLEN, :])
                al_hi[at * QLEN:(at + 1) * QLEN, :] = hi
                al_lo[at * QLEN:(at + 1) * QLEN, :] = lo

    r_hi, r_lo = split(1.0 / (eig[...].astype(F32) + DAMP))
    prod = mm(al_hi[...], r_hi, NN) + mm(al_lo[...], r_hi, NN) + mm(al_hi[...], r_lo, NN)
    width = eig.shape[1]
    for r in range(RANK):
        block = prod[r * HALF_TOK:(r + 1) * HALF_TOK] * b_ref[...]
        part[i, r * HALF_Q:(r + 1) * HALF_Q, :] = block.reshape(HALF_Q, QLEN, width).sum(axis=1)
    remote(part.at[i], recv.at[i], send_sem.at[i], recv_sem.at[i], partner).start()

    @pl.when(i == tiles - 1)
    def _():
        for j in range(tiles):
            remote(part.at[j], recv.at[j], send_sem.at[j], recv_sem.at[j], partner).wait()
            out[:, j * width:(j + 1) * width] = part[j] + recv[j]


def right_factors(left, a, eigval, b, width):
    own_rows, cols = eigval.shape
    tiles = cols // width
    toks = b.shape[0]
    dma = pltpu.SemaphoreType.DMA
    fixed = lambda i: (0, 0)
    return pl.pallas_call(
        functools.partial(right_kernel, tiles),
        grid=(tiles,),
        out_shape=jax.ShapeDtypeStruct((HALF_COLS, cols), F32),
        in_specs=[
            pl.BlockSpec((HALF_COLS, own_rows), fixed),
            pl.BlockSpec((toks, own_rows), fixed),
            pl.BlockSpec((own_rows, width), lambda i: (0, i)),
            pl.BlockSpec((toks, width), lambda i: (0, i)),
        ],
        out_specs=pl.BlockSpec((HALF_COLS, cols), fixed),
        scratch_shapes=[
            pltpu.VMEM((RANK * toks, own_rows), BF16), pltpu.VMEM((RANK * toks, own_rows), BF16),
            pltpu.VMEM((tiles, HALF_COLS, width), F32), pltpu.VMEM((tiles, HALF_COLS, width), F32),
            dma((tiles,)), dma((tiles,)),
        ],
        compiler_params=params(3),
    )(left, a, eigval, b)


def score_kernel(
    n, basis_in, right, left, basis_out, train_out, train_in, member, lens, owner, scores, totals,
    tile, part, recv, r_all, l_mine, l_theirs, l_all, proj, proj_theirs, src, src_recv, in_sem,
    rs_send, rs_recv, r_send, r_recv, l_send, l_recv, x_sem, s_send, s_recv,
):
    d = lax.axis_index("dp")
    p = lax.axis_index("pool")
    t = lax.axis_index("tensor")
    rows = tile.shape[1]
    out_rows = basis_out.shape[0]
    per_core = n // 2
    partner = {"tensor": 1 - t}
    peers = [lax.rem(d + k, n) for k in range(n)]
    others = [
        (q, k, {"pool": lax.rem(p + q, 2), "dp": peers[k]})
        for k in range(n) for q in range(2) if (q, k) != (0, 0)
    ]

    def fetch(s):
        to = lax.rem(d + 1 + s, n)
        return pltpu.make_async_copy(
            basis_in.at[pl.ds(pl.multiple_of(to * rows, rows), rows)], tile.at[s], in_sem.at[s]
        )

    for s in range(n):
        fetch(s).start()
    greet([target for _, _, target in others] + [partner])

    left_hi, left_lo = split(left[...])
    l_mine[...] = mm(left_hi, basis_out[...], NT) + mm(left_lo, basis_out[...], NT)
    holds = d // per_core == t
    handover = remote(l_mine, l_theirs, x_sem.at[0], x_sem.at[1], partner)

    @pl.when(jnp.logical_not(holds))
    def _():
        handover.start()

    right_hi, right_lo = split(right[...])
    pad = jnp.zeros_like(right_hi)
    stacked = jnp.concatenate([right_hi, right_lo, pad, pad], axis=0)

    def scatter(k):
        return remote(part.at[k - 1], recv.at[k], rs_send.at[k], rs_recv.at[k], {"dp": peers[k]})

    def step(s, carry):
        fetch(s).wait()
        prod = jnp.transpose(mm(tile[s], stacked, NT))
        part[s] = prod[:HALF_COLS] + prod[HALF_COLS:2 * HALF_COLS]

        @pl.when(s < n - 1)
        def _():
            to = lax.rem(d + 1 + s, n)
            remote(part.at[s], recv.at[s + 1], rs_send.at[s + 1], rs_recv.at[s + 1], {"dp": to}).start()

        return carry

    lax.fori_loop(0, n, step, 0)

    def left_copy(q, k, target, pool, index):
        return remote(
            l_all.at[p, lax.rem(d, per_core)], l_all.at[pool, index],
            l_send.at[q, k], l_recv.at[q, k], target,
        )

    @pl.when(holds)
    def _():
        handover.wait_recv()
        l_all[p, lax.rem(d, per_core)] = l_mine[...] + l_theirs[...]
        for q, k, target in others:
            left_copy(q, k, target, p, lax.rem(d, per_core)).start()

    total = part[n - 1]
    for k in range(1, n):
        scatter(k).wait_recv()
        total = total + recv[k]
    r_all[p, d] = total

    def right_copy(q, k, target, pool, index):
        return remote(r_all.at[p, d], r_all.at[pool, index], r_send.at[q, k], r_recv.at[q, k], target)

    for q, k, target in others:
        right_copy(q, k, target, p, d).start()

    for q, k, target in others:
        source = lax.rem(d + n - k, n)

        @pl.when(source // per_core == t)
        def _():
            left_copy(q, k, target, lax.rem(p + q, 2), lax.rem(source, per_core)).wait_recv()

    acc_out = [jnp.zeros((train_out.shape[0], HALF_COLS), F32) for _ in range(2)]
    for q in range(2):
        for c in range(per_core):
            hi, lo = split(l_all[q, c])
            x = train_out[:, c * out_rows:(c + 1) * out_rows]
            acc_out[q] = acc_out[q] + mm(x, hi, NT) + mm(x, lo, NT)
    for q in range(2):
        proj[q] = acc_out[q]

    for q, k, target in others:
        source = lax.rem(d + n - k, n)
        right_copy(q, k, target, lax.rem(p + q, 2), source).wait_recv()
    acc_in = [jnp.zeros((train_in.shape[0], HALF_COLS), F32) for _ in range(2)]
    for q in range(2):
        for c in range(n):
            hi, lo = split(r_all[q, c])
            x = train_in[:, c * rows:(c + 1) * rows]
            acc_in[q] = acc_in[q] + mm(x, hi, NT) + mm(x, lo, NT)
    for q in range(2):
        proj[2 + q] = acc_in[q]
    swap = remote(proj, proj_theirs, x_sem.at[2], x_sem.at[3], partner)
    swap.start()
    swap.wait()

    highest = lax.Precision.HIGHEST
    result = jnp.zeros(scores.shape, F32)
    for q in range(2):
        prod = (proj[q] + proj_theirs[q]) * (proj[2 + q] + proj_theirs[2 + q])
        by_col = jnp.dot(member[...], prod, precision=highest, preferred_element_type=F32)
        col = lax.broadcasted_iota(jnp.int32, (HALF_COLS, scores.shape[1]), 0)
        query = lax.broadcasted_iota(jnp.int32, (HALF_COLS, scores.shape[1]), 1)
        j = col % HALF_Q
        pick = (query == 2 * j + (j + q) % 2).astype(F32)
        result = result + jnp.dot(by_col, pick, precision=highest, preferred_element_type=F32)
    result = result / lens[...]
    scores[...] = result
    src[...] = jnp.dot(owner[...], result, precision=highest, preferred_element_type=F32)
    for k in range(1, n):
        remote(src, src_recv.at[k], s_send.at[k], s_recv.at[k], {"dp": peers[k]}).start()
    out = src[...]
    for k in range(1, n):
        remote(src, src_recv.at[k], s_send.at[k], s_recv.at[k], {"dp": peers[k]}).wait()
    for m in range(n):
        k = lax.rem(d - m + n, n)
        src_recv[0] = src[...]
        out = src_recv[k] if m == 0 else out + src_recv[k]
    totals[...] = out

    for k in range(1, n):
        scatter(k).wait_send()
    for q, k, target in others:
        right_copy(q, k, target, p, d).wait_send()

    @pl.when(holds)
    def _():
        for q, k, target in others:
            left_copy(q, k, target, p, lax.rem(d, per_core)).wait_send()

    @pl.when(jnp.logical_not(holds))
    def _():
        handover.wait_send()


def score(n, basis_in, right, left, basis_out, train_out, train_in, member, lens, owner):
    rows = basis_in.shape[0] // n
    toks = train_in.shape[0]
    out_rows = basis_out.shape[0]
    dma = pltpu.SemaphoreType.DMA
    vm = pltpu.VMEM
    return pl.pallas_call(
        functools.partial(score_kernel, n),
        out_shape=(
            jax.ShapeDtypeStruct((member.shape[0], 128), F32),
            jax.ShapeDtypeStruct((SOURCES, 128), F32),
        ),
        in_specs=[pl.BlockSpec(memory_space=pl.ANY)] + [VMEM] * 8,
        out_specs=(VMEM, VMEM),
        scratch_shapes=[
            vm((n, rows, basis_in.shape[1]), BF16),
            vm((n, HALF_COLS, rows), F32), vm((n, HALF_COLS, rows), F32),
            vm((2, n, HALF_COLS, rows), F32),
            vm((HALF_COLS, out_rows), F32), vm((HALF_COLS, out_rows), F32),
            vm((2, n // 2, HALF_COLS, out_rows), F32),
            vm((4, toks, HALF_COLS), F32), vm((4, toks, HALF_COLS), F32),
            vm((SOURCES, 128), F32), vm((n, SOURCES, 128), F32),
            dma((n,)), dma((n,)), dma((n,)), dma((2, n)), dma((2, n)), dma((2, n)), dma((2, n)),
            dma((4,)), dma((n,)), dma((n,)),
        ],
        compiler_params=params(4),
    )(basis_in, right, left, basis_out, train_out, train_in, member, lens, owner)


def body(
    n,
    train_out,
    train_in,
    query_out,
    query_in,
    basis_out,
    basis_in,
    eigval,
    sketch_bucket,
    sketch_sign,
    lengths,
    source_of_seq,
):
    p = lax.axis_index("pool")
    pairs = query_out.reshape(HALF_Q, 2, QLEN, query_out.shape[1])
    odd = ((jnp.arange(HALF_Q, dtype=jnp.int32) + p) % 2)[:, None, None]
    own_query_out = jnp.where(odd == 0, pairs[:, 0], pairs[:, 1]).reshape(HALF_TOK, -1)
    out_part = jnp.dot(own_query_out, basis_out, preferred_element_type=F32)
    q_all, a = gather(n, query_in, out_part)
    b = rotate(q_all, basis_in, 256)
    left = sketch_left(n, b, sketch_bucket[None], sketch_sign[None], eigval, a)
    right = right_factors(left, a, eigval, b, 256)

    seqs = lengths.shape[1]
    toks = train_out.shape[0]
    seq_len = lengths[0]
    seq_ends = jnp.cumsum(seq_len)
    seq_starts = seq_ends - seq_len
    positions = jnp.arange(toks, dtype=jnp.int32)
    member = (
        (positions[None, :] >= seq_starts[:, None]) & (positions[None, :] < seq_ends[:, None])
    ).astype(F32)
    pad_rows = 8 - seqs
    member = jnp.pad(member, ((0, pad_rows), (0, 0)))
    lens = jnp.pad(seq_len.astype(F32)[:, None], ((0, pad_rows), (0, 0)), constant_values=1.0)
    owner = (source_of_seq[None, :] == jnp.arange(SOURCES, dtype=jnp.int32)[:, None]).astype(F32)
    owner = jnp.pad(owner, ((0, 0), (0, pad_rows)))
    scores, totals = score(n, basis_in, right, left, basis_out, train_out, train_in, member, lens, owner)
    return (scores[:seqs, :QUERIES], totals[:, :QUERIES])


def sketch_table(bucket_ids, sign_bits):
    column_ids = jnp.arange(RANK, dtype=jnp.int32)
    signs = (2 * sign_bits - 1).astype(jnp.float32)
    return jnp.where(bucket_ids[:, None] == column_ids[None, :], signs[:, None], jnp.float32(0.0))


def seq_totals(proj_out, proj_in, seq_starts, seq_ends):
    token_score = (proj_out * proj_in).reshape(proj_out.shape[0], QUERIES, RANK).sum(axis=2)
    positions = jnp.arange(proj_out.shape[0], dtype=jnp.int32)
    member = (
        (positions[None, :] >= seq_starts[:, None]) & (positions[None, :] < seq_ends[:, None])
    ).astype(jnp.float32)
    return jnp.dot(member, token_score, precision=lax.Precision.HIGHEST)


def wide_body(
    train_out,
    train_in,
    query_out,
    query_in,
    basis_out,
    basis_in,
    eigval,
    sketch_bucket,
    sketch_sign,
    lengths,
    source_of_seq,
):
    factor_cols = QUERIES * RANK
    half_rows = basis_out.shape[1]
    own_cols = basis_in.shape[1]
    in_part = jnp.dot(
        lax.all_gather(query_in, "dp", axis=0, tiled=True),
        basis_in,
        preferred_element_type=jnp.float32,
    )
    out_part = lax.dot_general(
        basis_out, query_out, (((0,), (1,)), ((), ())), preferred_element_type=jnp.float32
    )
    rotated_out = lax.psum(out_part, "dp")
    rotated_in = lax.psum(in_part, "tensor")
    out_blocks = rotated_out.reshape(half_rows, QUERIES, QLEN)
    in_blocks = rotated_in.reshape(QUERIES, QLEN, own_cols)
    eig_plus = eigval.astype(jnp.float32) + DAMP
    precond = (
        jnp.einsum("eqi,qif->qef", out_blocks, in_blocks, precision=lax.Precision.HIGHEST)
        / eig_plus[None]
    )
    sketch = sketch_table(sketch_bucket, sketch_sign)
    sketch_part = jnp.einsum(
        "qef,fk->eqk", precond, sketch, precision=lax.Precision.HIGHEST
    ).reshape(half_rows, factor_cols)
    sketched = lax.psum(sketch_part, "dp").reshape(half_rows, QUERIES, RANK)
    gram_part = jnp.einsum("eqk,eql->qkl", sketched, sketched, precision=lax.Precision.HIGHEST)
    gram_matrix = lax.psum(gram_part, "tensor")
    chol_factor = jnp.linalg.cholesky(gram_matrix)
    left_trans = jax.scipy.linalg.solve_triangular(
        chol_factor, jnp.transpose(sketched, (1, 2, 0)), lower=True
    )
    right_part = jnp.einsum(
        "qef,qke->fqk", precond, left_trans, precision=lax.Precision.HIGHEST
    ).reshape(own_cols, factor_cols)
    left_eig = jnp.transpose(left_trans, (2, 0, 1)).reshape(half_rows, factor_cols)
    basis_out_wide = basis_out.astype(jnp.float32)
    left_part = jnp.dot(basis_out_wide, left_eig, precision=lax.Precision.HIGHEST)
    right_eig, left_mine = lax.psum((right_part, left_part), "tensor")
    basis_in_wide = basis_in.astype(jnp.float32)
    right_term = jnp.dot(basis_in_wide, right_eig, precision=lax.Precision.HIGHEST)
    right_full = lax.psum(right_term, "dp")
    left_full = lax.all_gather(left_mine, "dp", axis=0, tiled=True)
    core_index = lax.axis_index("tensor")
    left_half = lax.dynamic_slice_in_dim(left_full, core_index * half_rows, half_rows, 0)
    proj_out = jnp.dot(train_out.astype(jnp.float32), left_half, precision=lax.Precision.HIGHEST)
    proj_in = jnp.dot(train_in.astype(jnp.float32), right_full, precision=lax.Precision.HIGHEST)
    seq_len = lengths[0]
    seq_ends = jnp.cumsum(seq_len)
    seq_starts = seq_ends - seq_len
    out_whole, in_whole = lax.psum((proj_out, proj_in), "tensor")
    seq_sum = seq_totals(out_whole, in_whole, seq_starts, seq_ends)
    scores = seq_sum / seq_len.astype(jnp.float32)[:, None]
    owner_table = (source_of_seq[None, :] == jnp.arange(SOURCES, dtype=jnp.int32)[:, None]).astype(
        jnp.float32
    )
    source_part = jnp.dot(owner_table, scores, precision=lax.Precision.HIGHEST)
    source_totals = lax.psum(source_part, "dp")
    return (scores, source_totals)


def solution(mesh):
    n = mesh.shape["dp"]
    small = mesh.shape["pool"] == 2 and mesh.shape["tensor"] == 2 and n == QUERIES
    return jax.shard_map(
        functools.partial(body, n) if small else wide_body,
        mesh=mesh,
        in_specs=(
            P(("pool", "dp"), "tensor"),
            P(("pool", "dp"), "tensor"),
            P(None, "dp"),
            P("dp", "tensor"),
            P("dp", "tensor"),
            P("tensor", "dp"),
            P("tensor", "dp"),
            P("dp"),
            P("dp"),
            P(("pool", "dp"), None),
            P(("pool", "dp")),
        ),
        out_specs=(P(("pool", "dp"), None), P("pool", None)),
        check_vma=False,
    )
```

```python
import functools

import jax
import jax.numpy as jnp
from jax import lax
from jax.experimental import pallas as pl
from jax.experimental.pallas import tpu as pltpu
from jax.sharding import PartitionSpec as P

QUERIES = 8
QLEN = 16
RANK = 8
SOURCES = 32


DAMP = 0.1

F32 = jnp.float32
BF16 = jnp.bfloat16
MESH = pl.DeviceIdType.MESH
NT = (((1,), (1,)), ((), ()))
NN = (((1,), (0,)), ((), ()))
HALF_Q = QUERIES // 2
HALF_TOK = HALF_Q * QLEN
HALF_COLS = HALF_Q * RANK
VMEM = pl.BlockSpec(memory_space=pltpu.VMEM)


def split(x):
    hi = x.astype(BF16)
    return hi, (x - hi.astype(F32)).astype(BF16)


def mm(a, b, dims):
    return lax.dot_general(a, b, dims, preferred_element_type=F32)


def greet(targets):
    barrier = pltpu.get_barrier_semaphore()
    for target in targets:
        pl.semaphore_signal(barrier, inc=1, device_id=target, device_id_type=MESH)
    pl.semaphore_wait(barrier, len(targets))


def remote(src, dst, send, recv, target):
    return pltpu.make_async_remote_copy(
        src_ref=src, dst_ref=dst, send_sem=send, recv_sem=recv,
        device_id=target, device_id_type=MESH,
    )


def params(collective_id):
    return pltpu.CompilerParams(
        collective_id=collective_id, has_side_effects=True, vmem_limit_bytes=56 << 20
    )


def other_devices(n):
    d = lax.axis_index("dp")
    p = lax.axis_index("pool")
    return [
        (q, k, {"pool": lax.rem(p + q, 2), "dp": lax.rem(d + k, n)})
        for k in range(n) for q in range(2) if (q, k) != (0, 0)
    ]


def gather_kernel(zs, qin, qout, basis, q_all, part, z_send, z_recv, x_send, x_recv):
    d = lax.axis_index("dp")
    p = lax.axis_index("pool")
    z, x = d // 2, d % 2
    across = {"dp": 2 * z + 1 - x}
    greet([{"dp": 2 * lax.rem(z + k, zs) + x} for k in range(1, zs)] + [across])
    own = pl.ds(pl.multiple_of(z * QLEN, QLEN), QLEN)
    is_sender = x == lax.rem(z + p, 2)

    def along(k):
        return remote(qin, q_all.at[own], z_send.at[k], z_recv.at[z], {"dp": 2 * lax.rem(z + k, zs) + x})

    def over(j):
        rows = q_all.at[j * QLEN:(j + 1) * QLEN]
        return remote(rows, rows, x_send.at[j], x_recv.at[j], across)

    @pl.when(is_sender)
    def _():
        for k in range(1, zs):
            along(k).start()
        q_all[own, :] = qin[...]

    part[...] = mm(qout[...], basis[...], NN)
    for j in range(zs):
        in_column = x == lax.rem(j + p, 2)

        @pl.when(jnp.logical_and(in_column, z != j))
        def _():
            rows = q_all.at[j * QLEN:(j + 1) * QLEN]
            remote(qin, rows, z_send.at[0], z_recv.at[j], across).wait_recv()

        @pl.when(in_column)
        def _():
            over(j).start()

    for j in range(zs):
        in_column = x == lax.rem(j + p, 2)

        @pl.when(in_column)
        def _():
            over(j).wait_send()

        @pl.when(jnp.logical_not(in_column))
        def _():
            over(j).wait_recv()

    @pl.when(is_sender)
    def _():
        for k in range(1, zs):
            along(k).wait_send()


def gather(n, query_in, query_out, basis_out):
    dma = pltpu.SemaphoreType.DMA
    zs = n // 2
    return pl.pallas_call(
        functools.partial(gather_kernel, zs),
        out_shape=(
            jax.ShapeDtypeStruct((HALF_TOK, query_in.shape[1]), BF16),
            jax.ShapeDtypeStruct((HALF_TOK, basis_out.shape[1]), F32),
        ),
        in_specs=[VMEM] * 3,
        out_specs=(VMEM, VMEM),
        scratch_shapes=[dma((zs,)), dma((zs,)), dma((zs,)), dma((zs,))],
        compiler_params=params(0),
    )(query_in, query_out, basis_out)


def rotate_kernel(
    n, tiles, q_all, basis, a_in, out, a_out, part, recv, a_part, a_sum, a_recv, send_sem, recv_sem,
    rs_send, rs_recv, ag_send, ag_recv,
):
    i = pl.program_id(0)
    d = lax.axis_index("dp")
    partner = {"tensor": 1 - lax.axis_index("tensor")}
    peers = [lax.rem(d + k, n) for k in range(n)]
    rows = a_part.shape[0] // n
    own = pl.ds(pl.multiple_of(d * rows, rows), rows)

    def scatter(k):
        return remote(
            a_part.at[pl.ds(pl.multiple_of(peers[k] * rows, rows), rows)], a_recv.at[k],
            rs_send.at[k], rs_recv.at[k], {"dp": peers[k]},
        )

    def share(k, source):
        theirs = pl.ds(pl.multiple_of(source * rows, rows), rows)
        return remote(a_sum.at[own], a_sum.at[theirs], ag_send.at[k], ag_recv.at[k], {"dp": peers[k]})

    @pl.when(i == 0)
    def _():
        greet([partner] + [{"dp": peers[k]} for k in range(1, n)])
        a_part[...] = a_in[...]
        for k in range(1, n):
            scatter(k).start()

    part[i] = mm(q_all[...], basis[...], NN)
    remote(part.at[i], recv.at[i], send_sem.at[i], recv_sem.at[i], partner).start()

    @pl.when(i == tiles // 2)
    def _():
        total = a_part[own, :]
        for k in range(1, n):
            scatter(k).wait_recv()
            total = total + a_recv[k]
        a_sum[own, :] = total
        for k in range(1, n):
            share(k, d).start()

    @pl.when(i == tiles - 1)
    def _():
        width = part.shape[2]
        for j in range(tiles):
            remote(part.at[j], recv.at[j], send_sem.at[j], recv_sem.at[j], partner).wait()
            out[:, j * width:(j + 1) * width] = part[j] + recv[j]
        for k in range(1, n):
            share(k, lax.rem(d + n - k, n)).wait()
            scatter(k).wait_send()
        a_out[...] = a_sum[...]


def rotate(n, q_all, basis_in, a_part, width):
    depth, cols = basis_in.shape
    rows = q_all.shape[0]
    tiles = cols // width
    dma = pltpu.SemaphoreType.DMA
    fixed = lambda i: (0, 0)
    return pl.pallas_call(
        functools.partial(rotate_kernel, n, tiles),
        grid=(tiles,),
        out_shape=(
            jax.ShapeDtypeStruct((rows, cols), F32),
            jax.ShapeDtypeStruct(a_part.shape, F32),
        ),
        in_specs=[
            pl.BlockSpec((rows, depth), fixed),
            pl.BlockSpec((depth, width), lambda i: (0, i)),
            VMEM,
        ],
        out_specs=(pl.BlockSpec((rows, cols), fixed), VMEM),
        scratch_shapes=[
            pltpu.VMEM((tiles, rows, width), F32), pltpu.VMEM((tiles, rows, width), F32),
            pltpu.VMEM(a_part.shape, F32), pltpu.VMEM(a_part.shape, F32),
            pltpu.VMEM((n, a_part.shape[0] // n, a_part.shape[1]), F32),
            dma((tiles,)), dma((tiles,)), dma((n,)), dma((n,)), dma((n,)), dma((n,)),
        ],
        compiler_params=params(1),
    )(q_all, basis_in, a_part)


def sketch_kernel(
    n, b_ref, bucket, sign, eig, a_ref, left, bs_hi, bs_lo, part, recv, whole, gram_mine, gram_theirs,
    rs_send, rs_recv, ag_send, ag_recv, g_sem,
):
    i = pl.program_id(0)
    d = lax.axis_index("dp")
    partner = {"tensor": 1 - lax.axis_index("tensor")}

    @pl.when(i == 0)
    def _():
        greet([{"dp": lax.rem(d + k, n)} for k in range(1, n)] + [partner])
        signs = (2 * sign[...] - 1).astype(F32)
        for k in range(RANK):
            table = jnp.where(bucket[...] == k, signs, 0.0)
            hi, lo = split(b_ref[...] * table)
            bs_hi[k * HALF_TOK:(k + 1) * HALF_TOK, :] = hi
            bs_lo[k * HALF_TOK:(k + 1) * HALF_TOK, :] = lo

    r_hi, r_lo = split(1.0 / (eig[...].astype(F32) + DAMP))
    prod = mm(bs_hi[...], r_hi, NT) + mm(bs_lo[...], r_hi, NT) + mm(bs_hi[...], r_lo, NT)
    width = eig.shape[0]
    for k in range(RANK):
        block = prod[k * HALF_TOK:(k + 1) * HALF_TOK] * a_ref[...]
        part[i, k * HALF_Q:(k + 1) * HALF_Q, :] = block.reshape(HALF_Q, QLEN, width).sum(axis=1)

    def scatter(k):
        to = lax.rem(d + k, n)
        return remote(part.at[to], recv.at[k], rs_send.at[k], rs_recv.at[k], {"dp": to})

    @pl.when(i != d)
    def _():
        k = lax.rem(i - d + n, n)
        remote(part.at[i], recv.at[k], rs_send.at[k], rs_recv.at[k], {"dp": i}).start()

    @pl.when(i == n - 1)
    def _():
        total = part[d]
        for k in range(1, n):
            scatter(k).wait_recv()
            total = total + recv[k]
        whole[d] = total
        for k in range(1, n):
            to = lax.rem(d + k, n)
            remote(whole.at[d], whole.at[d], ag_send.at[k], ag_recv.at[k], {"dp": to}).start()
        for k in range(1, n):
            to, source = lax.rem(d + k, n), lax.rem(d + n - k, n)
            remote(whole.at[d], whole.at[source], ag_send.at[k], ag_recv.at[k], {"dp": to}).wait()
            scatter(k).wait_send()
        rows = [
            jnp.concatenate([whole[c, k * HALF_Q:(k + 1) * HALF_Q, :] for c in range(n)], axis=1)
            for k in range(RANK)
        ]
        lane = lax.broadcasted_iota(jnp.int32, (HALF_Q, 128), 1)
        packed = jnp.zeros((HALF_Q, 128), F32)
        for r in range(RANK):
            for k in range(r + 1):
                dot = jnp.sum(rows[r] * rows[k], axis=1, keepdims=True)
                packed = jnp.where(lane == r * RANK + k, dot, packed)
        gram_mine[0:HALF_Q, :] = packed
        gram_mine[HALF_Q:2 * HALF_Q, :] = packed
        copy = remote(gram_mine, gram_theirs, g_sem.at[0], g_sem.at[1], partner)
        copy.start()
        copy.wait()
        gram = gram_mine[0:HALF_Q, :] + gram_theirs[0:HALF_Q, :]
        low = [[None] * RANK for _ in range(RANK)]
        done = []
        for r in range(RANK):
            for k in range(r + 1):
                value = gram[:, r * RANK + k:r * RANK + k + 1]
                for m in range(k):
                    value = value - low[r][m] * low[k][m]
                low[r][k] = jnp.sqrt(value) if k == r else value / low[k][k]
            row = rows[r]
            for k in range(r):
                row = row - low[r][k] * done[k]
            row = row / low[r][r]
            done.append(row)
            left[r * HALF_Q:(r + 1) * HALF_Q, :] = row


def sketch_left(n, b, bucket, sign, eigval, a):
    own_rows, cols = eigval.shape
    width = own_rows // n
    toks = b.shape[0]
    dma = pltpu.SemaphoreType.DMA
    fixed = lambda i: (0, 0)
    return pl.pallas_call(
        functools.partial(sketch_kernel, n),
        grid=(n,),
        out_shape=jax.ShapeDtypeStruct((HALF_COLS, own_rows), F32),
        in_specs=[
            pl.BlockSpec((toks, cols), fixed),
            pl.BlockSpec((1, cols), fixed),
            pl.BlockSpec((1, cols), fixed),
            pl.BlockSpec((width, cols), lambda i: (i, 0)),
            pl.BlockSpec((toks, width), lambda i: (0, i)),
        ],
        out_specs=pl.BlockSpec((HALF_COLS, own_rows), fixed),
        scratch_shapes=[
            pltpu.VMEM((RANK * toks, cols), BF16), pltpu.VMEM((RANK * toks, cols), BF16),
            pltpu.VMEM((n, HALF_COLS, width), F32), pltpu.VMEM((n, HALF_COLS, width), F32),
            pltpu.VMEM((n, HALF_COLS, width), F32),
            pltpu.VMEM((2 * HALF_Q, 128), F32), pltpu.VMEM((2 * HALF_Q, 128), F32),
            dma((n,)), dma((n,)), dma((n,)), dma((n,)), dma((2,)),
        ],
        compiler_params=params(2),
    )(b, bucket, sign, eigval, a)


def right_kernel(
    n, tiles, left, a_ref, basis_out, eig, b_ref, out, l_out, al_hi, al_lo, part, recv, l_mine, l_theirs, l_all,
    send_sem, recv_sem, l_send, l_recv, x_sem,
):
    i = pl.program_id(0)
    d = lax.axis_index("dp")
    p = lax.axis_index("pool")
    t = lax.axis_index("tensor")
    partner = {"tensor": 1 - t}
    per_core = n // 2
    others = other_devices(n)
    holds = d // per_core == t
    handover = remote(l_mine, l_theirs, x_sem.at[0], x_sem.at[1], partner)

    def left_copy(q, k, target, pool, index):
        return remote(
            l_all.at[p, lax.rem(d, per_core)], l_all.at[pool, index],
            l_send.at[q, k], l_recv.at[q, k], target,
        )

    @pl.when(i == 0)
    def _():
        greet([target for _, _, target in others] + [partner])
        left_hi, left_lo = split(left[...])
        l_mine[...] = mm(left_hi, basis_out[...], NT) + mm(left_lo, basis_out[...], NT)

        @pl.when(jnp.logical_not(holds))
        def _():
            handover.start()

        for r in range(RANK):
            for j in range(HALF_Q):
                at = r * HALF_Q + j
                hi, lo = split(left[at:at + 1, :] * a_ref[j * QLEN:(j + 1) * QLEN, :])
                al_hi[at * QLEN:(at + 1) * QLEN, :] = hi
                al_lo[at * QLEN:(at + 1) * QLEN, :] = lo

    r_hi, r_lo = split(1.0 / (eig[...].astype(F32) + DAMP))
    prod = mm(al_hi[...], r_hi, NN) + mm(al_lo[...], r_hi, NN) + mm(al_hi[...], r_lo, NN)
    width = eig.shape[1]
    for r in range(RANK):
        block = prod[r * HALF_TOK:(r + 1) * HALF_TOK] * b_ref[...]
        part[i, r * HALF_Q:(r + 1) * HALF_Q, :] = block.reshape(HALF_Q, QLEN, width).sum(axis=1)
    remote(part.at[i], recv.at[i], send_sem.at[i], recv_sem.at[i], partner).start()

    @pl.when(jnp.logical_and(i == 0, holds))
    def _():
        handover.wait_recv()
        l_all[p, lax.rem(d, per_core)] = l_mine[...] + l_theirs[...]
        for q, k, target in others:
            left_copy(q, k, target, p, lax.rem(d, per_core)).start()

    @pl.when(i == tiles - 1)
    def _():
        for q, k, target in others:
            source = lax.rem(d + n - k, n)

            @pl.when(source // per_core == t)
            def _():
                left_copy(q, k, target, lax.rem(p + q, 2), lax.rem(source, per_core)).wait_recv()

            @pl.when(holds)
            def _():
                left_copy(q, k, target, p, lax.rem(d, per_core)).wait_send()

        @pl.when(jnp.logical_not(holds))
        def _():
            handover.wait_send()

        l_out[...] = l_all[...]
        for j in range(tiles):
            remote(part.at[j], recv.at[j], send_sem.at[j], recv_sem.at[j], partner).wait()
            out[:, j * width:(j + 1) * width] = part[j] + recv[j]


def right_factors(n, left, a, basis_out, eigval, b, width):
    own_rows, cols = eigval.shape
    tiles = cols // width
    toks = b.shape[0]
    dma = pltpu.SemaphoreType.DMA
    fixed = lambda i: (0, 0)
    return pl.pallas_call(
        functools.partial(right_kernel, n, tiles),
        grid=(tiles,),
        out_shape=(
            jax.ShapeDtypeStruct((HALF_COLS, cols), F32),
            jax.ShapeDtypeStruct((2, n // 2, HALF_COLS, basis_out.shape[0]), F32),
        ),
        in_specs=[
            pl.BlockSpec((HALF_COLS, own_rows), fixed),
            pl.BlockSpec((toks, own_rows), fixed),
            VMEM,
            pl.BlockSpec((own_rows, width), lambda i: (0, i)),
            pl.BlockSpec((toks, width), lambda i: (0, i)),
        ],
        out_specs=(pl.BlockSpec((HALF_COLS, cols), fixed), VMEM),
        scratch_shapes=[
            pltpu.VMEM((RANK * toks, own_rows), BF16), pltpu.VMEM((RANK * toks, own_rows), BF16),
            pltpu.VMEM((tiles, HALF_COLS, width), F32), pltpu.VMEM((tiles, HALF_COLS, width), F32),
            pltpu.VMEM((HALF_COLS, basis_out.shape[0]), F32),
            pltpu.VMEM((HALF_COLS, basis_out.shape[0]), F32),
            pltpu.VMEM((2, n // 2, HALF_COLS, basis_out.shape[0]), F32),
            dma((tiles,)), dma((tiles,)), dma((2, n)), dma((2, n)), dma((2,)),
        ],
        compiler_params=params(3),
    )(left, a, basis_out, eigval, b)


def score_kernel(
    n, basis_in, right, l_all, train_out, train_in, member, lens, owner, scores, totals,
    tile, part, recv_x, recv_z, r_all, proj, proj_theirs, src, src_recv, in_sem,
    xs_send, xs_recv, zs_send, zs_recv, z_send, z_recv, x_send, x_recv, y_send, y_recv, w_send, w_recv,
    t_sem, s_send, s_recv,
):
    d = lax.axis_index("dp")
    p = lax.axis_index("pool")
    rows = tile.shape[1]
    out_rows = l_all.shape[3]
    zs = n // 2
    z, x = d // 2, d % 2
    partner = {"tensor": 1 - lax.axis_index("tensor")}
    across = {"dp": 2 * z + 1 - x}
    beside = {"pool": 1 - p}
    peers = [lax.rem(d + k, n) for k in range(n)]
    up = [{"dp": 2 * lax.rem(z + k, zs) + x} for k in range(zs)]

    def fetch(s):
        side = jnp.where(s < zs, 1 - x, x)
        to = 2 * lax.rem(z + 1 + s, zs) + side
        return pltpu.make_async_copy(
            basis_in.at[pl.ds(pl.multiple_of(to * rows, rows), rows)], tile.at[s], in_sem.at[s]
        )

    for s in range(n):
        fetch(s).start()
    greet([{"dp": peers[k]} for k in range(1, n)] + [beside, partner])

    right_hi, right_lo = split(right[...])
    pad = jnp.zeros_like(right_hi)
    stacked = jnp.concatenate([right_hi, right_lo, pad, pad], axis=0)

    def share(s):
        fetch(s).wait()
        prod = jnp.transpose(mm(tile[s], stacked, NT))
        return prod[:HALF_COLS] + prod[HALF_COLS:2 * HALF_COLS]

    def pass_over(s):
        return remote(part.at[s], recv_x.at[s], xs_send.at[s], xs_recv.at[s], across)

    def pass_along(m, target):
        return remote(part.at[zs + m], recv_z.at[m], zs_send.at[m], zs_recv.at[m], target)

    def first(s, carry):
        part[s] = share(s)
        pass_over(s).start()
        return carry

    lax.fori_loop(0, zs, first, 0)

    def second(m, carry):
        mine = share(zs + m)
        pass_over(m).wait_recv()
        part[zs + m] = mine + recv_x[m]

        @pl.when(m < zs - 1)
        def _():
            pass_along(m, {"dp": 2 * lax.rem(z + 1 + m, zs) + x}).start()

        return carry

    lax.fori_loop(0, zs, second, 0)

    acc_out = [jnp.zeros((train_out.shape[0], HALF_COLS), F32) for _ in range(2)]
    for q in range(2):
        for c in range(zs):
            hi, lo = split(l_all[q, c])
            cols = train_out[:, c * out_rows:(c + 1) * out_rows]
            acc_out[q] = acc_out[q] + mm(cols, hi, NT) + mm(cols, lo, NT)
        proj[q] = acc_out[q]

    total = part[n - 1]
    for m in range(zs - 1):
        pass_along(m, up[m + 1]).wait_recv()
        total = total + recv_z[m]
    r_all[p, d] = total

    def block(pool, k, side):
        return r_all.at[pool, 2 * lax.rem(z + zs - k, zs) + side]

    def along(k, source):
        return remote(r_all.at[p, d], source, z_send.at[k], z_recv.at[k], up[k])

    def over(k, side):
        return remote(block(p, k, side), block(p, k, side), x_send.at[k], x_recv.at[k], across)

    def cross(k, pool):
        return remote(block(pool, k, x), block(pool, k, x), y_send.at[k], y_recv.at[k], beside)

    def corner(k, sending):
        if k < zs // 2:
            ref = block(1 - p, k, x if sending else 1 - x)
            return remote(ref, ref, w_send.at[k], w_recv.at[k], across)
        ref = block(p if sending else 1 - p, k, 1 - x)
        return remote(ref, ref, w_send.at[k], w_recv.at[k], beside)

    for k in range(1, zs):
        along(k, r_all.at[p, d]).start()
    for k in range(zs):
        if k:
            along(k, block(p, k, x)).wait_recv()
        over(k, x).start()
        cross(k, p).start()
    acc_in = [jnp.zeros((train_in.shape[0], HALF_COLS), F32) for _ in range(2)]

    def project(q, pool_at, dp_at, acc):
        hi, lo = split(r_all[pool_at, dp_at])
        cols = train_in[:, pl.ds(pl.multiple_of(dp_at * rows, rows), rows)]
        return acc + mm(cols, hi, NT) + mm(cols, lo, NT)

    for k in range(zs):
        if k < zs // 2:
            cross(k, 1 - p).wait_recv()
            corner(k, True).start()
            over(k, 1 - x).wait_recv()
        else:
            over(k, 1 - x).wait_recv()
            corner(k, True).start()
            cross(k, 1 - p).wait_recv()
    for k in range(zs):
        at = 2 * lax.rem(z + zs - k, zs)
        acc_in[0] = project(0, p, at + x, acc_in[0])
        acc_in[0] = project(0, p, at + 1 - x, acc_in[0])
        acc_in[1] = project(1, 1 - p, at + x, acc_in[1])
    for k in range(zs):
        at = 2 * lax.rem(z + zs - k, zs)
        corner(k, False).wait_recv()
        acc_in[1] = project(1, 1 - p, at + 1 - x, acc_in[1])
    for q in range(2):
        proj[2 + q] = jnp.where(p == q, acc_in[0], acc_in[1])
    swap = remote(proj, proj_theirs, t_sem.at[0], t_sem.at[1], partner)
    swap.start()
    swap.wait()

    highest = lax.Precision.HIGHEST
    result = jnp.zeros(scores.shape, F32)
    for q in range(2):
        prod = (proj[q] + proj_theirs[q]) * (proj[2 + q] + proj_theirs[2 + q])
        by_col = jnp.dot(member[...], prod, precision=highest, preferred_element_type=F32)
        col = lax.broadcasted_iota(jnp.int32, (HALF_COLS, scores.shape[1]), 0)
        query = lax.broadcasted_iota(jnp.int32, (HALF_COLS, scores.shape[1]), 1)
        j = col % HALF_Q
        pick = (query == 2 * j + (j + q) % 2).astype(F32)
        result = result + jnp.dot(by_col, pick, precision=highest, preferred_element_type=F32)
    result = result / lens[...]
    scores[...] = result
    src[...] = jnp.dot(owner[...], result, precision=highest, preferred_element_type=F32)
    for k in range(1, n):
        remote(src, src_recv.at[k], s_send.at[k], s_recv.at[k], {"dp": peers[k]}).start()
    out = src[...]
    for k in range(1, n):
        remote(src, src_recv.at[k], s_send.at[k], s_recv.at[k], {"dp": peers[k]}).wait()
    for m in range(n):
        k = lax.rem(d - m + n, n)
        src_recv[0] = src[...]
        out = src_recv[k] if m == 0 else out + src_recv[k]
    totals[...] = out

    for k in range(zs):
        pass_over(k).wait_send()
        over(k, x).wait_send()
        cross(k, p).wait_send()
        corner(k, True).wait_send()
    for k in range(1, zs):
        pass_along(k - 1, up[k]).wait_send()
        along(k, r_all.at[p, d]).wait_send()


def score(n, basis_in, right, l_all, train_out, train_in, member, lens, owner):
    rows = basis_in.shape[0] // n
    toks = train_in.shape[0]
    zs = n // 2
    dma = pltpu.SemaphoreType.DMA
    vm = pltpu.VMEM
    return pl.pallas_call(
        functools.partial(score_kernel, n),
        out_shape=(
            jax.ShapeDtypeStruct((member.shape[0], 128), F32),
            jax.ShapeDtypeStruct((SOURCES, 128), F32),
        ),
        in_specs=[pl.BlockSpec(memory_space=pl.ANY)] + [VMEM] * 7,
        out_specs=(VMEM, VMEM),
        scratch_shapes=[
            vm((n, rows, basis_in.shape[1]), BF16),
            vm((n, HALF_COLS, rows), F32),
            vm((zs, HALF_COLS, rows), F32), vm((zs, HALF_COLS, rows), F32),
            vm((2, n, HALF_COLS, rows), F32),
            vm((4, toks, HALF_COLS), F32), vm((4, toks, HALF_COLS), F32),
            vm((SOURCES, 128), F32), vm((n, SOURCES, 128), F32),
            dma((n,)), *[dma((zs,)) for _ in range(12)], dma((2,)), dma((n,)), dma((n,)),
        ],
        compiler_params=params(4),
    )(basis_in, right, l_all, train_out, train_in, member, lens, owner)


def body(
    n,
    train_out,
    train_in,
    query_out,
    query_in,
    basis_out,
    basis_in,
    eigval,
    sketch_bucket,
    sketch_sign,
    lengths,
    source_of_seq,
):
    p = lax.axis_index("pool")
    pairs = query_out.reshape(HALF_Q, 2, QLEN, query_out.shape[1])
    odd = ((jnp.arange(HALF_Q, dtype=jnp.int32) + p) % 2)[:, None, None]
    own_query_out = jnp.where(odd == 0, pairs[:, 0], pairs[:, 1]).reshape(HALF_TOK, -1)
    q_all, a_part = gather(n, query_in, own_query_out, basis_out)
    b, a = rotate(n, q_all, basis_in, a_part, 256)
    left = sketch_left(n, b, sketch_bucket[None], sketch_sign[None], eigval, a)
    right, l_all = right_factors(n, left, a, basis_out, eigval, b, 256)

    seqs = lengths.shape[1]
    toks = train_out.shape[0]
    seq_len = lengths[0]
    seq_ends = jnp.cumsum(seq_len)
    seq_starts = seq_ends - seq_len
    positions = jnp.arange(toks, dtype=jnp.int32)
    member = (
        (positions[None, :] >= seq_starts[:, None]) & (positions[None, :] < seq_ends[:, None])
    ).astype(F32)
    pad_rows = 8 - seqs
    member = jnp.pad(member, ((0, pad_rows), (0, 0)))
    lens = jnp.pad(seq_len.astype(F32)[:, None], ((0, pad_rows), (0, 0)), constant_values=1.0)
    owner = (source_of_seq[None, :] == jnp.arange(SOURCES, dtype=jnp.int32)[:, None]).astype(F32)
    owner = jnp.pad(owner, ((0, 0), (0, pad_rows)))
    scores, totals = score(n, basis_in, right, l_all, train_out, train_in, member, lens, owner)
    return (scores[:seqs, :QUERIES], totals[:, :QUERIES])


def sketch_table(bucket_ids, sign_bits):
    column_ids = jnp.arange(RANK, dtype=jnp.int32)
    signs = (2 * sign_bits - 1).astype(jnp.float32)
    return jnp.where(bucket_ids[:, None] == column_ids[None, :], signs[:, None], jnp.float32(0.0))


def seq_totals(proj_out, proj_in, seq_starts, seq_ends):
    token_score = (proj_out * proj_in).reshape(proj_out.shape[0], QUERIES, RANK).sum(axis=2)
    positions = jnp.arange(proj_out.shape[0], dtype=jnp.int32)
    member = (
        (positions[None, :] >= seq_starts[:, None]) & (positions[None, :] < seq_ends[:, None])
    ).astype(jnp.float32)
    return jnp.dot(member, token_score, precision=lax.Precision.HIGHEST)


def wide_body(
    train_out,
    train_in,
    query_out,
    query_in,
    basis_out,
    basis_in,
    eigval,
    sketch_bucket,
    sketch_sign,
    lengths,
    source_of_seq,
):
    factor_cols = QUERIES * RANK
    half_rows = basis_out.shape[1]
    own_cols = basis_in.shape[1]
    in_part = jnp.dot(
        lax.all_gather(query_in, "dp", axis=0, tiled=True),
        basis_in,
        preferred_element_type=jnp.float32,
    )
    out_part = lax.dot_general(
        basis_out, query_out, (((0,), (1,)), ((), ())), preferred_element_type=jnp.float32
    )
    rotated_out = lax.psum(out_part, "dp")
    rotated_in = lax.psum(in_part, "tensor")
    out_blocks = rotated_out.reshape(half_rows, QUERIES, QLEN)
    in_blocks = rotated_in.reshape(QUERIES, QLEN, own_cols)
    eig_plus = eigval.astype(jnp.float32) + DAMP
    precond = (
        jnp.einsum("eqi,qif->qef", out_blocks, in_blocks, precision=lax.Precision.HIGHEST)
        / eig_plus[None]
    )
    sketch = sketch_table(sketch_bucket, sketch_sign)
    sketch_part = jnp.einsum(
        "qef,fk->eqk", precond, sketch, precision=lax.Precision.HIGHEST
    ).reshape(half_rows, factor_cols)
    sketched = lax.psum(sketch_part, "dp").reshape(half_rows, QUERIES, RANK)
    gram_part = jnp.einsum("eqk,eql->qkl", sketched, sketched, precision=lax.Precision.HIGHEST)
    gram_matrix = lax.psum(gram_part, "tensor")
    chol_factor = jnp.linalg.cholesky(gram_matrix)
    left_trans = jax.scipy.linalg.solve_triangular(
        chol_factor, jnp.transpose(sketched, (1, 2, 0)), lower=True
    )
    right_part = jnp.einsum(
        "qef,qke->fqk", precond, left_trans, precision=lax.Precision.HIGHEST
    ).reshape(own_cols, factor_cols)
    left_eig = jnp.transpose(left_trans, (2, 0, 1)).reshape(half_rows, factor_cols)
    basis_out_wide = basis_out.astype(jnp.float32)
    left_part = jnp.dot(basis_out_wide, left_eig, precision=lax.Precision.HIGHEST)
    right_eig, left_mine = lax.psum((right_part, left_part), "tensor")
    basis_in_wide = basis_in.astype(jnp.float32)
    right_term = jnp.dot(basis_in_wide, right_eig, precision=lax.Precision.HIGHEST)
    right_full = lax.psum(right_term, "dp")
    left_full = lax.all_gather(left_mine, "dp", axis=0, tiled=True)
    core_index = lax.axis_index("tensor")
    left_half = lax.dynamic_slice_in_dim(left_full, core_index * half_rows, half_rows, 0)
    proj_out = jnp.dot(train_out.astype(jnp.float32), left_half, precision=lax.Precision.HIGHEST)
    proj_in = jnp.dot(train_in.astype(jnp.float32), right_full, precision=lax.Precision.HIGHEST)
    seq_len = lengths[0]
    seq_ends = jnp.cumsum(seq_len)
    seq_starts = seq_ends - seq_len
    out_whole, in_whole = lax.psum((proj_out, proj_in), "tensor")
    seq_sum = seq_totals(out_whole, in_whole, seq_starts, seq_ends)
    scores = seq_sum / seq_len.astype(jnp.float32)[:, None]
    owner_table = (source_of_seq[None, :] == jnp.arange(SOURCES, dtype=jnp.int32)[:, None]).astype(
        jnp.float32
    )
    source_part = jnp.dot(owner_table, scores, precision=lax.Precision.HIGHEST)
    source_totals = lax.psum(source_part, "dp")
    return (scores, source_totals)


def solution(mesh):
    n = mesh.shape["dp"]
    small = mesh.shape["pool"] == 2 and mesh.shape["tensor"] == 2 and n == QUERIES
    return jax.shard_map(
        functools.partial(body, n) if small else wide_body,
        mesh=mesh,
        in_specs=(
            P(("pool", "dp"), "tensor"),
            P(("pool", "dp"), "tensor"),
            P(None, "dp"),
            P("dp", "tensor"),
            P("dp", "tensor"),
            P("tensor", "dp"),
            P("tensor", "dp"),
            P("dp"),
            P("dp"),
            P(("pool", "dp"), None),
            P(("pool", "dp")),
        ),
        out_specs=(P(("pool", "dp"), None), P("pool", None)),
        check_vma=False,
    )
```

```python
import functools

import jax
import jax.numpy as jnp
from jax import lax
from jax.experimental import pallas as pl
from jax.experimental.pallas import tpu as pltpu
from jax.sharding import PartitionSpec as P

QUERIES = 8
QLEN = 16
RANK = 8
SOURCES = 32


DAMP = 0.1

F32 = jnp.float32
BF16 = jnp.bfloat16
MESH = pl.DeviceIdType.MESH
NT = (((1,), (1,)), ((), ()))
NN = (((1,), (0,)), ((), ()))
HALF_Q = QUERIES // 2
HALF_TOK = HALF_Q * QLEN
HALF_COLS = HALF_Q * RANK
VMEM = pl.BlockSpec(memory_space=pltpu.VMEM)


def split(x):
    hi = x.astype(BF16)
    return hi, (x - hi.astype(F32)).astype(BF16)


def mm(a, b, dims):
    return lax.dot_general(a, b, dims, preferred_element_type=F32)


def greet(targets):
    barrier = pltpu.get_barrier_semaphore()
    for target in targets:
        pl.semaphore_signal(barrier, inc=1, device_id=target, device_id_type=MESH)
    pl.semaphore_wait(barrier, len(targets))


def remote(src, dst, send, recv, target):
    return pltpu.make_async_remote_copy(
        src_ref=src, dst_ref=dst, send_sem=send, recv_sem=recv,
        device_id=target, device_id_type=MESH,
    )


def params(collective_id):
    return pltpu.CompilerParams(
        collective_id=collective_id, has_side_effects=True, vmem_limit_bytes=56 << 20
    )


def other_devices(n):
    d = lax.axis_index("dp")
    p = lax.axis_index("pool")
    return [
        (q, k, {"pool": lax.rem(p + q, 2), "dp": lax.rem(d + k, n)})
        for k in range(n) for q in range(2) if (q, k) != (0, 0)
    ]


def gather_kernel(zs, qin, qout, basis, q_all, part, z_send, z_recv, x_send, x_recv):
    d = lax.axis_index("dp")
    p = lax.axis_index("pool")
    z, x = d // 2, d % 2
    across = {"dp": 2 * z + 1 - x}
    greet([{"dp": 2 * lax.rem(z + k, zs) + x} for k in range(1, zs)] + [across])
    own = pl.ds(pl.multiple_of(z * QLEN, QLEN), QLEN)
    is_sender = x == lax.rem(z + p, 2)

    halves = 2
    width = qin.shape[1] // halves

    def columns(h):
        return pl.ds(h * width, width)

    def along(k, h):
        return remote(
            qin.at[:, columns(h)], q_all.at[own, columns(h)], z_send.at[h, k], z_recv.at[h, z],
            {"dp": 2 * lax.rem(z + k, zs) + x},
        )

    def over(j, h):
        rows = q_all.at[j * QLEN:(j + 1) * QLEN, columns(h)]
        return remote(rows, rows, x_send.at[h, j], x_recv.at[h, j], across)

    @pl.when(is_sender)
    def _():
        for h in range(halves):
            for k in range(1, zs):
                along(k, h).start()
        q_all[own, :] = qin[...]

    def forward(j, h, local):
        in_column = x == lax.rem(j + p, 2)

        @pl.when(jnp.logical_and(in_column, (z == j) if local else (z != j)))
        def _():
            if not local:
                rows = q_all.at[j * QLEN:(j + 1) * QLEN, columns(h)]
                remote(qin.at[:, columns(h)], rows, z_send.at[h, 0], z_recv.at[h, j], across).wait_recv()
            over(j, h).start()

    for j in range(zs):
        for h in range(halves):
            forward(j, h, True)
    part[...] = mm(qout[...], basis[...], NN)
    for h in range(halves):
        for j in range(zs):
            forward(j, h, False)

    for j in range(zs):
        in_column = x == lax.rem(j + p, 2)

        @pl.when(in_column)
        def _():
            for h in range(halves):
                over(j, h).wait_send()

        @pl.when(jnp.logical_not(in_column))
        def _():
            for h in range(halves):
                over(j, h).wait_recv()

    @pl.when(is_sender)
    def _():
        for h in range(halves):
            for k in range(1, zs):
                along(k, h).wait_send()


def gather(n, query_in, query_out, basis_out):
    dma = pltpu.SemaphoreType.DMA
    zs = n // 2
    return pl.pallas_call(
        functools.partial(gather_kernel, zs),
        out_shape=(
            jax.ShapeDtypeStruct((HALF_TOK, query_in.shape[1]), BF16),
            jax.ShapeDtypeStruct((HALF_TOK, basis_out.shape[1]), F32),
        ),
        in_specs=[VMEM] * 3,
        out_specs=(VMEM, VMEM),
        scratch_shapes=[dma((2, zs)) for _ in range(4)],
        compiler_params=params(0),
    )(query_in, query_out, basis_out)


def rotate_kernel(
    n, tiles, q_all, basis, a_in, out, a_out, part, recv, a_part, a_recv, send_sem, recv_sem,
    rs_send, rs_recv,
):
    i = pl.program_id(0)
    d = lax.axis_index("dp")
    partner = {"tensor": 1 - lax.axis_index("tensor")}
    peers = [lax.rem(d + k, n) for k in range(n)]
    rows = a_part.shape[0] // n
    own = pl.ds(pl.multiple_of(d * rows, rows), rows)

    def scatter(k):
        return remote(
            a_part.at[pl.ds(pl.multiple_of(peers[k] * rows, rows), rows)], a_recv.at[k],
            rs_send.at[k], rs_recv.at[k], {"dp": peers[k]},
        )

    @pl.when(i == 0)
    def _():
        greet([partner] + [{"dp": peers[k]} for k in range(1, n)])
        a_part[...] = a_in[...]
        for k in range(1, n):
            scatter(k).start()

    part[i] = mm(q_all[...], basis[...], NN)
    remote(part.at[i], recv.at[i], send_sem.at[i], recv_sem.at[i], partner).start()

    @pl.when(i == tiles - 1)
    def _():
        width = part.shape[2]
        for j in range(tiles):
            remote(part.at[j], recv.at[j], send_sem.at[j], recv_sem.at[j], partner).wait()
            out[:, j * width:(j + 1) * width] = part[j] + recv[j]
        total = a_part[own, :]
        for k in range(1, n):
            scatter(k).wait()
            total = total + a_recv[k]
        a_out[...] = total


def rotate(n, q_all, basis_in, a_part, width):
    depth, cols = basis_in.shape
    rows = q_all.shape[0]
    tiles = cols // width
    dma = pltpu.SemaphoreType.DMA
    fixed = lambda i: (0, 0)
    return pl.pallas_call(
        functools.partial(rotate_kernel, n, tiles),
        grid=(tiles,),
        out_shape=(
            jax.ShapeDtypeStruct((rows, cols), F32),
            jax.ShapeDtypeStruct((a_part.shape[0] // n, a_part.shape[1]), F32),
        ),
        in_specs=[
            pl.BlockSpec((rows, depth), fixed),
            pl.BlockSpec((depth, width), lambda i: (0, i)),
            VMEM,
        ],
        out_specs=(pl.BlockSpec((rows, cols), fixed), VMEM),
        scratch_shapes=[
            pltpu.VMEM((tiles, rows, width), F32), pltpu.VMEM((tiles, rows, width), F32),
            pltpu.VMEM(a_part.shape, F32),
            pltpu.VMEM((n, a_part.shape[0] // n, a_part.shape[1]), F32),
            dma((tiles,)), dma((tiles,)), dma((n,)), dma((n,)),
        ],
        compiler_params=params(1),
    )(q_all, basis_in, a_part)


def sketch_kernel(
    n, b_ref, bucket, sign, eig, a_own, left, a_out, bs_hi, bs_lo, prods, a_sum, part, recv, whole,
    gram_mine, gram_theirs, a_send, a_recv, rs_send, rs_recv, ag_send, ag_recv, g_sem,
):
    i = pl.program_id(0)
    d = lax.axis_index("dp")
    partner = {"tensor": 1 - lax.axis_index("tensor")}

    a_rows = a_own.shape[0]
    own = pl.ds(pl.multiple_of(d * a_rows, a_rows), a_rows)

    def a_copy(k, source):
        theirs = pl.ds(pl.multiple_of(source * a_rows, a_rows), a_rows)
        return remote(
            a_sum.at[own], a_sum.at[theirs], a_send.at[k], a_recv.at[k], {"dp": lax.rem(d + k, n)}
        )

    @pl.when(i == 0)
    def _():
        greet([{"dp": lax.rem(d + k, n)} for k in range(1, n)] + [partner])
        a_sum[own, :] = a_own[...]
        for k in range(1, n):
            a_copy(k, d).start()
        signs = (2 * sign[...] - 1).astype(F32)
        for k in range(RANK):
            table = jnp.where(bucket[...] == k, signs, 0.0)
            hi, lo = split(b_ref[...] * table)
            bs_hi[k * HALF_TOK:(k + 1) * HALF_TOK, :] = hi
            bs_lo[k * HALF_TOK:(k + 1) * HALF_TOK, :] = lo

    r_hi, r_lo = split(1.0 / (eig[...].astype(F32) + DAMP))
    prods[i] = mm(bs_hi[...], r_hi, NT) + mm(bs_lo[...], r_hi, NT) + mm(bs_hi[...], r_lo, NT)
    width = eig.shape[0]

    def scatter(k):
        to = lax.rem(d + k, n)
        return remote(part.at[to], recv.at[k], rs_send.at[k], rs_recv.at[k], {"dp": to})

    @pl.when(i == n - 1)
    def _():
        for k in range(1, n):
            a_copy(k, lax.rem(d + n - k, n)).wait()
        for c in range(n):
            columns = a_sum[:, c * width:(c + 1) * width]
            for k in range(RANK):
                block = prods[c, k * HALF_TOK:(k + 1) * HALF_TOK, :] * columns
                part[c, k * HALF_Q:(k + 1) * HALF_Q, :] = block.reshape(HALF_Q, QLEN, width).sum(axis=1)

            @pl.when(d != c)
            def _():
                k = lax.rem(c - d + n, n)
                remote(part.at[c], recv.at[k], rs_send.at[k], rs_recv.at[k], {"dp": c}).start()

        a_out[...] = a_sum[...]
        total = part[d]
        for k in range(1, n):
            scatter(k).wait_recv()
            total = total + recv[k]
        whole[d] = total
        for k in range(1, n):
            to = lax.rem(d + k, n)
            remote(whole.at[d], whole.at[d], ag_send.at[k], ag_recv.at[k], {"dp": to}).start()
        for k in range(1, n):
            to, source = lax.rem(d + k, n), lax.rem(d + n - k, n)
            remote(whole.at[d], whole.at[source], ag_send.at[k], ag_recv.at[k], {"dp": to}).wait()
            scatter(k).wait_send()
        rows = [
            jnp.concatenate([whole[c, k * HALF_Q:(k + 1) * HALF_Q, :] for c in range(n)], axis=1)
            for k in range(RANK)
        ]
        lane = lax.broadcasted_iota(jnp.int32, (HALF_Q, 128), 1)
        packed = jnp.zeros((HALF_Q, 128), F32)
        for r in range(RANK):
            for k in range(r + 1):
                dot = jnp.sum(rows[r] * rows[k], axis=1, keepdims=True)
                packed = jnp.where(lane == r * RANK + k, dot, packed)
        gram_mine[0:HALF_Q, :] = packed
        gram_mine[HALF_Q:2 * HALF_Q, :] = packed
        copy = remote(gram_mine, gram_theirs, g_sem.at[0], g_sem.at[1], partner)
        copy.start()
        copy.wait()
        gram = gram_mine[0:HALF_Q, :] + gram_theirs[0:HALF_Q, :]
        low = [[None] * RANK for _ in range(RANK)]
        done, inverse = [], []
        for r in range(RANK):
            for k in range(r + 1):
                value = gram[:, r * RANK + k:r * RANK + k + 1]
                for m in range(k):
                    value = value - low[r][m] * low[k][m]
                low[r][k] = jnp.sqrt(value) if k == r else value * inverse[k]
            inverse.append(1.0 / low[r][r])
            row = rows[r]
            for k in range(r):
                row = row - low[r][k] * done[k]
            row = row * inverse[r]
            done.append(row)
            left[r * HALF_Q:(r + 1) * HALF_Q, :] = row


def sketch_left(n, b, bucket, sign, eigval, a):
    own_rows, cols = eigval.shape
    width = own_rows // n
    toks = b.shape[0]
    dma = pltpu.SemaphoreType.DMA
    fixed = lambda i: (0, 0)
    return pl.pallas_call(
        functools.partial(sketch_kernel, n),
        grid=(n,),
        out_shape=(
            jax.ShapeDtypeStruct((HALF_COLS, own_rows), F32),
            jax.ShapeDtypeStruct((toks, own_rows), F32),
        ),
        in_specs=[
            pl.BlockSpec((toks, cols), fixed),
            pl.BlockSpec((1, cols), fixed),
            pl.BlockSpec((1, cols), fixed),
            pl.BlockSpec((width, cols), lambda i: (i, 0)),
            pl.BlockSpec(a.shape, fixed),
        ],
        out_specs=(pl.BlockSpec((HALF_COLS, own_rows), fixed), pl.BlockSpec((toks, own_rows), fixed)),
        scratch_shapes=[
            pltpu.VMEM((RANK * toks, cols), BF16), pltpu.VMEM((RANK * toks, cols), BF16),
            pltpu.VMEM((n, RANK * toks, width), F32), pltpu.VMEM((toks, own_rows), F32),
            pltpu.VMEM((n, HALF_COLS, width), F32), pltpu.VMEM((n, HALF_COLS, width), F32),
            pltpu.VMEM((n, HALF_COLS, width), F32),
            pltpu.VMEM((2 * HALF_Q, 128), F32), pltpu.VMEM((2 * HALF_Q, 128), F32),
            *[dma((n,)) for _ in range(6)], dma((2,)),
        ],
        compiler_params=params(2),
    )(b, bucket, sign, eigval, a)


def right_kernel(
    n, tiles, left, a_ref, basis_out, eig, b_ref, out, l_out, al_hi, al_lo, part, recv, l_mine, l_theirs, l_all,
    send_sem, recv_sem, l_send, l_recv, x_sem,
):
    i = pl.program_id(0)
    d = lax.axis_index("dp")
    p = lax.axis_index("pool")
    t = lax.axis_index("tensor")
    partner = {"tensor": 1 - t}
    per_core = n // 2
    others = other_devices(n)
    holds = d // per_core == t
    handover = remote(l_mine, l_theirs, x_sem.at[0], x_sem.at[1], partner)

    def left_copy(q, k, target, pool, index):
        return remote(
            l_all.at[p, lax.rem(d, per_core)], l_all.at[pool, index],
            l_send.at[q, k], l_recv.at[q, k], target,
        )

    @pl.when(i == 0)
    def _():
        greet([target for _, _, target in others] + [partner])
        left_hi, left_lo = split(left[...])
        l_mine[...] = mm(left_hi, basis_out[...], NT) + mm(left_lo, basis_out[...], NT)

        @pl.when(jnp.logical_not(holds))
        def _():
            handover.start()

        for r in range(RANK):
            for j in range(HALF_Q):
                at = r * HALF_Q + j
                hi, lo = split(left[at:at + 1, :] * a_ref[j * QLEN:(j + 1) * QLEN, :])
                al_hi[at * QLEN:(at + 1) * QLEN, :] = hi
                al_lo[at * QLEN:(at + 1) * QLEN, :] = lo

    r_hi, r_lo = split(1.0 / (eig[...].astype(F32) + DAMP))
    prod = mm(al_hi[...], r_hi, NN) + mm(al_lo[...], r_hi, NN) + mm(al_hi[...], r_lo, NN)
    width = eig.shape[1]
    for r in range(RANK):
        block = prod[r * HALF_TOK:(r + 1) * HALF_TOK] * b_ref[...]
        part[i, r * HALF_Q:(r + 1) * HALF_Q, :] = block.reshape(HALF_Q, QLEN, width).sum(axis=1)
    remote(part.at[i], recv.at[i], send_sem.at[i], recv_sem.at[i], partner).start()

    @pl.when(jnp.logical_and(i == 0, holds))
    def _():
        handover.wait_recv()
        l_all[p, lax.rem(d, per_core)] = l_mine[...] + l_theirs[...]
        for q, k, target in others:
            left_copy(q, k, target, p, lax.rem(d, per_core)).start()

    @pl.when(i == tiles - 1)
    def _():
        for q, k, target in others:
            source = lax.rem(d + n - k, n)

            @pl.when(source // per_core == t)
            def _():
                left_copy(q, k, target, lax.rem(p + q, 2), lax.rem(source, per_core)).wait_recv()

            @pl.when(holds)
            def _():
                left_copy(q, k, target, p, lax.rem(d, per_core)).wait_send()

        @pl.when(jnp.logical_not(holds))
        def _():
            handover.wait_send()

        l_out[...] = l_all[...]
        for j in range(tiles):
            remote(part.at[j], recv.at[j], send_sem.at[j], recv_sem.at[j], partner).wait()
            out[:, j * width:(j + 1) * width] = part[j] + recv[j]


def right_factors(n, left, a, basis_out, eigval, b, width):
    own_rows, cols = eigval.shape
    tiles = cols // width
    toks = b.shape[0]
    dma = pltpu.SemaphoreType.DMA
    fixed = lambda i: (0, 0)
    return pl.pallas_call(
        functools.partial(right_kernel, n, tiles),
        grid=(tiles,),
        out_shape=(
            jax.ShapeDtypeStruct((HALF_COLS, cols), F32),
            jax.ShapeDtypeStruct((2, n // 2, HALF_COLS, basis_out.shape[0]), F32),
        ),
        in_specs=[
            pl.BlockSpec((HALF_COLS, own_rows), fixed),
            pl.BlockSpec((toks, own_rows), fixed),
            VMEM,
            pl.BlockSpec((own_rows, width), lambda i: (0, i)),
            pl.BlockSpec((toks, width), lambda i: (0, i)),
        ],
        out_specs=(pl.BlockSpec((HALF_COLS, cols), fixed), VMEM),
        scratch_shapes=[
            pltpu.VMEM((RANK * toks, own_rows), BF16), pltpu.VMEM((RANK * toks, own_rows), BF16),
            pltpu.VMEM((tiles, HALF_COLS, width), F32), pltpu.VMEM((tiles, HALF_COLS, width), F32),
            pltpu.VMEM((HALF_COLS, basis_out.shape[0]), F32),
            pltpu.VMEM((HALF_COLS, basis_out.shape[0]), F32),
            pltpu.VMEM((2, n // 2, HALF_COLS, basis_out.shape[0]), F32),
            dma((tiles,)), dma((tiles,)), dma((2, n)), dma((2, n)), dma((2,)),
        ],
        compiler_params=params(3),
    )(left, a, basis_out, eigval, b)


def score_kernel(
    n, basis_in, right, l_all, train_out, train_in, member, lens, owner, scores, totals,
    tile, part, recv_x, recv_z, r_all, proj, proj_theirs, src, src_recv, in_sem,
    xs_send, xs_recv, zs_send, zs_recv, z_send, z_recv, x_send, x_recv, y_send, y_recv, w_send, w_recv,
    t_sem, s_send, s_recv,
):
    d = lax.axis_index("dp")
    p = lax.axis_index("pool")
    rows = tile.shape[1]
    out_rows = l_all.shape[3]
    zs = n // 2
    z, x = d // 2, d % 2
    partner = {"tensor": 1 - lax.axis_index("tensor")}
    across = {"dp": 2 * z + 1 - x}
    beside = {"pool": 1 - p}
    peers = [lax.rem(d + k, n) for k in range(n)]
    up = [{"dp": 2 * lax.rem(z + k, zs) + x} for k in range(zs)]

    def fetch(s):
        side = jnp.where(s < zs, 1 - x, x)
        to = 2 * lax.rem(z + 1 + s, zs) + side
        return pltpu.make_async_copy(
            basis_in.at[pl.ds(pl.multiple_of(to * rows, rows), rows)], tile.at[s], in_sem.at[s]
        )

    for s in range(n):
        fetch(s).start()
    greet([{"dp": peers[k]} for k in range(1, n)] + [beside, partner])

    right_hi, right_lo = split(right[...])
    pad = jnp.zeros_like(right_hi)
    stacked = jnp.concatenate([right_hi, right_lo, pad, pad], axis=0)

    def share(s):
        fetch(s).wait()
        prod = jnp.transpose(mm(tile[s], stacked, NT))
        return prod[:HALF_COLS] + prod[HALF_COLS:2 * HALF_COLS]

    def pass_over(s):
        return remote(part.at[s], recv_x.at[s], xs_send.at[s], xs_recv.at[s], across)

    def pass_along(m, target):
        return remote(part.at[zs + m], recv_z.at[m], zs_send.at[m], zs_recv.at[m], target)

    def first(s, carry):
        part[s] = share(s)
        pass_over(s).start()
        return carry

    lax.fori_loop(0, zs, first, 0)

    def second(m, carry):
        mine = share(zs + m)
        pass_over(m).wait_recv()
        part[zs + m] = mine + recv_x[m]

        @pl.when(m < zs - 1)
        def _():
            pass_along(m, {"dp": 2 * lax.rem(z + 1 + m, zs) + x}).start()

        return carry

    lax.fori_loop(0, zs, second, 0)

    acc_out = [jnp.zeros((train_out.shape[0], HALF_COLS), F32) for _ in range(2)]
    for q in range(2):
        for c in range(zs):
            hi, lo = split(l_all[q, c])
            cols = train_out[:, c * out_rows:(c + 1) * out_rows]
            acc_out[q] = acc_out[q] + mm(cols, hi, NT) + mm(cols, lo, NT)
        proj[q] = acc_out[q]

    total = part[n - 1]
    for m in range(zs - 1):
        pass_along(m, up[m + 1]).wait_recv()
        total = total + recv_z[m]
    r_all[p, d] = total

    def block(pool, k, side):
        return r_all.at[pool, 2 * lax.rem(z + zs - k, zs) + side]

    def along(k, source):
        return remote(r_all.at[p, d], source, z_send.at[k], z_recv.at[k], up[k])

    def over(k, side):
        return remote(block(p, k, side), block(p, k, side), x_send.at[k], x_recv.at[k], across)

    def cross(k, pool):
        return remote(block(pool, k, x), block(pool, k, x), y_send.at[k], y_recv.at[k], beside)

    def corner(k, sending):
        if k < zs // 2:
            ref = block(1 - p, k, x if sending else 1 - x)
            return remote(ref, ref, w_send.at[k], w_recv.at[k], across)
        ref = block(p if sending else 1 - p, k, 1 - x)
        return remote(ref, ref, w_send.at[k], w_recv.at[k], beside)

    for k in range(1, zs):
        along(k, r_all.at[p, d]).start()
    for k in range(zs):
        if k:
            along(k, block(p, k, x)).wait_recv()
        over(k, x).start()
        cross(k, p).start()
    acc_in = [jnp.zeros((train_in.shape[0], HALF_COLS), F32) for _ in range(2)]

    def project(q, pool_at, dp_at, acc):
        hi, lo = split(r_all[pool_at, dp_at])
        cols = train_in[:, pl.ds(pl.multiple_of(dp_at * rows, rows), rows)]
        return acc + mm(cols, hi, NT) + mm(cols, lo, NT)

    for k in range(zs):
        if k < zs // 2:
            cross(k, 1 - p).wait_recv()
            corner(k, True).start()
            over(k, 1 - x).wait_recv()
        else:
            over(k, 1 - x).wait_recv()
            corner(k, True).start()
            cross(k, 1 - p).wait_recv()
    for k in range(zs):
        at = 2 * lax.rem(z + zs - k, zs)
        acc_in[0] = project(0, p, at + x, acc_in[0])
        acc_in[0] = project(0, p, at + 1 - x, acc_in[0])
        acc_in[1] = project(1, 1 - p, at + x, acc_in[1])
    for k in range(zs):
        at = 2 * lax.rem(z + zs - k, zs)
        corner(k, False).wait_recv()
        acc_in[1] = project(1, 1 - p, at + 1 - x, acc_in[1])
    for q in range(2):
        proj[2 + q] = jnp.where(p == q, acc_in[0], acc_in[1])
    swap = remote(proj, proj_theirs, t_sem.at[0], t_sem.at[1], partner)
    swap.start()
    swap.wait()

    highest = lax.Precision.HIGHEST
    result = jnp.zeros((member.shape[0], 128), F32)
    for q in range(2):
        prod = (proj[q] + proj_theirs[q]) * (proj[2 + q] + proj_theirs[2 + q])
        by_col = jnp.dot(member[...], prod, precision=highest, preferred_element_type=F32)
        col = lax.broadcasted_iota(jnp.int32, (HALF_COLS, 128), 0)
        query = lax.broadcasted_iota(jnp.int32, (HALF_COLS, 128), 1)
        j = col % HALF_Q
        pick = (query == 2 * j + (j + q) % 2).astype(F32)
        result = result + jnp.dot(by_col, pick, precision=highest, preferred_element_type=F32)
    result = result / lens[...]
    scores[...] = result[:scores.shape[0], :QUERIES]
    src[...] = jnp.dot(owner[...], result, precision=highest, preferred_element_type=F32)
    for k in range(1, n):
        remote(src, src_recv.at[k], s_send.at[k], s_recv.at[k], {"dp": peers[k]}).start()
    out = src[...]
    for k in range(1, n):
        remote(src, src_recv.at[k], s_send.at[k], s_recv.at[k], {"dp": peers[k]}).wait()
    for m in range(n):
        k = lax.rem(d - m + n, n)
        src_recv[0] = src[...]
        out = src_recv[k] if m == 0 else out + src_recv[k]
    totals[...] = out[:, :QUERIES]

    for k in range(zs):
        pass_over(k).wait_send()
        over(k, x).wait_send()
        cross(k, p).wait_send()
        corner(k, True).wait_send()
    for k in range(1, zs):
        pass_along(k - 1, up[k]).wait_send()
        along(k, r_all.at[p, d]).wait_send()


def score(n, seqs, basis_in, right, l_all, train_out, train_in, member, lens, owner):
    rows = basis_in.shape[0] // n
    toks = train_in.shape[0]
    zs = n // 2
    dma = pltpu.SemaphoreType.DMA
    vm = pltpu.VMEM
    return pl.pallas_call(
        functools.partial(score_kernel, n),
        out_shape=(
            jax.ShapeDtypeStruct((seqs, QUERIES), F32),
            jax.ShapeDtypeStruct((SOURCES, QUERIES), F32),
        ),
        in_specs=[pl.BlockSpec(memory_space=pl.ANY)] + [VMEM] * 7,
        out_specs=(VMEM, VMEM),
        scratch_shapes=[
            vm((n, rows, basis_in.shape[1]), BF16),
            vm((n, HALF_COLS, rows), F32),
            vm((zs, HALF_COLS, rows), F32), vm((zs, HALF_COLS, rows), F32),
            vm((2, n, HALF_COLS, rows), F32),
            vm((4, toks, HALF_COLS), F32), vm((4, toks, HALF_COLS), F32),
            vm((SOURCES, 128), F32), vm((n, SOURCES, 128), F32),
            dma((n,)), *[dma((zs,)) for _ in range(12)], dma((2,)), dma((n,)), dma((n,)),
        ],
        compiler_params=params(4),
    )(basis_in, right, l_all, train_out, train_in, member, lens, owner)


def body(
    n,
    train_out,
    train_in,
    query_out,
    query_in,
    basis_out,
    basis_in,
    eigval,
    sketch_bucket,
    sketch_sign,
    lengths,
    source_of_seq,
):
    p = lax.axis_index("pool")
    pairs = query_out.reshape(HALF_Q, 2, QLEN, query_out.shape[1])
    odd = ((jnp.arange(HALF_Q, dtype=jnp.int32) + p) % 2)[:, None, None]
    own_query_out = jnp.where(odd == 0, pairs[:, 0], pairs[:, 1]).reshape(HALF_TOK, -1)
    q_all, a_part = gather(n, query_in, own_query_out, basis_out)
    b, a_own = rotate(n, q_all, basis_in, a_part, 256)
    left, a = sketch_left(n, b, sketch_bucket[None], sketch_sign[None], eigval, a_own)
    right, l_all = right_factors(n, left, a, basis_out, eigval, b, 256)

    seqs = lengths.shape[1]
    toks = train_out.shape[0]
    seq_len = lengths[0]
    seq_ends = jnp.cumsum(seq_len)
    seq_starts = seq_ends - seq_len
    positions = jnp.arange(toks, dtype=jnp.int32)
    member = (
        (positions[None, :] >= seq_starts[:, None]) & (positions[None, :] < seq_ends[:, None])
    ).astype(F32)
    pad_rows = 8 - seqs
    member = jnp.pad(member, ((0, pad_rows), (0, 0)))
    lens = jnp.pad(seq_len.astype(F32)[:, None], ((0, pad_rows), (0, 0)), constant_values=1.0)
    owner = (source_of_seq[None, :] == jnp.arange(SOURCES, dtype=jnp.int32)[:, None]).astype(F32)
    owner = jnp.pad(owner, ((0, 0), (0, pad_rows)))
    return score(n, seqs, basis_in, right, l_all, train_out, train_in, member, lens, owner)


def sketch_table(bucket_ids, sign_bits):
    column_ids = jnp.arange(RANK, dtype=jnp.int32)
    signs = (2 * sign_bits - 1).astype(jnp.float32)
    return jnp.where(bucket_ids[:, None] == column_ids[None, :], signs[:, None], jnp.float32(0.0))


def seq_totals(proj_out, proj_in, seq_starts, seq_ends):
    token_score = (proj_out * proj_in).reshape(proj_out.shape[0], QUERIES, RANK).sum(axis=2)
    positions = jnp.arange(proj_out.shape[0], dtype=jnp.int32)
    member = (
        (positions[None, :] >= seq_starts[:, None]) & (positions[None, :] < seq_ends[:, None])
    ).astype(jnp.float32)
    return jnp.dot(member, token_score, precision=lax.Precision.HIGHEST)


def wide_body(
    train_out,
    train_in,
    query_out,
    query_in,
    basis_out,
    basis_in,
    eigval,
    sketch_bucket,
    sketch_sign,
    lengths,
    source_of_seq,
):
    factor_cols = QUERIES * RANK
    half_rows = basis_out.shape[1]
    own_cols = basis_in.shape[1]
    in_part = jnp.dot(
        lax.all_gather(query_in, "dp", axis=0, tiled=True),
        basis_in,
        preferred_element_type=jnp.float32,
    )
    out_part = lax.dot_general(
        basis_out, query_out, (((0,), (1,)), ((), ())), preferred_element_type=jnp.float32
    )
    rotated_out = lax.psum(out_part, "dp")
    rotated_in = lax.psum(in_part, "tensor")
    out_blocks = rotated_out.reshape(half_rows, QUERIES, QLEN)
    in_blocks = rotated_in.reshape(QUERIES, QLEN, own_cols)
    eig_plus = eigval.astype(jnp.float32) + DAMP
    precond = (
        jnp.einsum("eqi,qif->qef", out_blocks, in_blocks, precision=lax.Precision.HIGHEST)
        / eig_plus[None]
    )
    sketch = sketch_table(sketch_bucket, sketch_sign)
    sketch_part = jnp.einsum(
        "qef,fk->eqk", precond, sketch, precision=lax.Precision.HIGHEST
    ).reshape(half_rows, factor_cols)
    sketched = lax.psum(sketch_part, "dp").reshape(half_rows, QUERIES, RANK)
    gram_part = jnp.einsum("eqk,eql->qkl", sketched, sketched, precision=lax.Precision.HIGHEST)
    gram_matrix = lax.psum(gram_part, "tensor")
    chol_factor = jnp.linalg.cholesky(gram_matrix)
    left_trans = jax.scipy.linalg.solve_triangular(
        chol_factor, jnp.transpose(sketched, (1, 2, 0)), lower=True
    )
    right_part = jnp.einsum(
        "qef,qke->fqk", precond, left_trans, precision=lax.Precision.HIGHEST
    ).reshape(own_cols, factor_cols)
    left_eig = jnp.transpose(left_trans, (2, 0, 1)).reshape(half_rows, factor_cols)
    basis_out_wide = basis_out.astype(jnp.float32)
    left_part = jnp.dot(basis_out_wide, left_eig, precision=lax.Precision.HIGHEST)
    right_eig, left_mine = lax.psum((right_part, left_part), "tensor")
    basis_in_wide = basis_in.astype(jnp.float32)
    right_term = jnp.dot(basis_in_wide, right_eig, precision=lax.Precision.HIGHEST)
    right_full = lax.psum(right_term, "dp")
    left_full = lax.all_gather(left_mine, "dp", axis=0, tiled=True)
    core_index = lax.axis_index("tensor")
    left_half = lax.dynamic_slice_in_dim(left_full, core_index * half_rows, half_rows, 0)
    proj_out = jnp.dot(train_out.astype(jnp.float32), left_half, precision=lax.Precision.HIGHEST)
    proj_in = jnp.dot(train_in.astype(jnp.float32), right_full, precision=lax.Precision.HIGHEST)
    seq_len = lengths[0]
    seq_ends = jnp.cumsum(seq_len)
    seq_starts = seq_ends - seq_len
    out_whole, in_whole = lax.psum((proj_out, proj_in), "tensor")
    seq_sum = seq_totals(out_whole, in_whole, seq_starts, seq_ends)
    scores = seq_sum / seq_len.astype(jnp.float32)[:, None]
    owner_table = (source_of_seq[None, :] == jnp.arange(SOURCES, dtype=jnp.int32)[:, None]).astype(
        jnp.float32
    )
    source_part = jnp.dot(owner_table, scores, precision=lax.Precision.HIGHEST)
    source_totals = lax.psum(source_part, "dp")
    return (scores, source_totals)


def solution(mesh):
    n = mesh.shape["dp"]
    small = mesh.shape["pool"] == 2 and mesh.shape["tensor"] == 2 and n == QUERIES
    return jax.shard_map(
        functools.partial(body, n) if small else wide_body,
        mesh=mesh,
        in_specs=(
            P(("pool", "dp"), "tensor"),
            P(("pool", "dp"), "tensor"),
            P(None, "dp"),
            P("dp", "tensor"),
            P("dp", "tensor"),
            P("tensor", "dp"),
            P("tensor", "dp"),
            P("dp"),
            P("dp"),
            P(("pool", "dp"), None),
            P(("pool", "dp")),
        ),
        out_specs=(P(("pool", "dp"), None), P("pool", None)),
        check_vma=False,
    )
```
